128 devices in a mesh: sec: 2 (over z_lo), grp: 4 (over z_hi, core), tp: 16 (over y, x).
Axes of the slice: x: 4, y: 4, z: 4 (z_hi: 2, z_lo: 2; z = z_hi * 2 + z_lo), core: 2. Of those that a mesh axis runs over, the one named last changes fastest.
Arguments:
- queries: bfloat16 [128, 4, 8192], P(('grp', 'tp'), None, 'sec'), may hold values from -80 to 80
- new_token_pairs: bfloat16 [128, 4, 2, 1024], P(('grp', 'tp'), None, None, 'sec'), may hold values from -4 to 4
- paged_cache_store: bfloat16 [6144, 64, 2, 1024], P(('grp', 'tp'), None, None, 'sec'), may hold values from -5 to 5
- page_table: int32 [128, 48], P(('grp', 'tp')), may hold values from 0 to 95, as said below
- cache_lengths: int32 [128], P(('grp', 'tp')), may hold values from 1 to 3072
- out_weight: bfloat16 [8192, 8192], P('sec', ('grp', 'tp')), may hold values from -0.5 to 0.5
- residual: bfloat16 [512, 8192], P(None, ('grp', 'tp')), may hold values from -32 to 32
- norm_gain: float32 [8192], replicated, may hold values from 0.5 to 1.5
- gate_weight: bfloat16 [28672, 8192], P(('sec', 'grp', 'tp')), may hold values from -0.0625 to 0.0625
- up_weight: bfloat16 [28672, 8192], P(('sec', 'grp', 'tp')), may hold values from -0.0625 to 0.0625
- down_weight: bfloat16 [28672, 8192], P(('sec', 'grp', 'tp')), may hold values from -0.125 to 0.125
Outputs:
- layer_output: bfloat16 [512, 8192], P(None, ('grp', 'tp'))
The draws below stay inside these ranges and needn't reach their ends.
Inputs may be any that keep to these rules, and one draw needn't show every extreme that they name: `page_table`: the rows of the 2 requests of one aligned block name each of that block's 96 pages exactly once.
All inputs are finite; a program needn't handle non-finite values.
Results may differ from the reference program's by a relative error of at most 0.01.
Values may be sent and summed in bfloat16 or wider, within the bound.
A program may use at most 128 MiB of HBM per device.

```python
import jax
import jax.numpy as jnp
from jax import lax

D = 8192
FF = 28672
QUERY_HEADS = 64
KEY_VALUE_HEADS = 8
HEAD_SIZE = 128
QUERY_TOKENS = 4
PAGE_TOKENS = 64
MAXLEN = 3072
REQ_DEV = 2
MAXPAGES = 48
PAGES_DEV = 96
REQUEST_COUNT = 128
ROWS = 512
POOL_PAGES = 6144


def shared_keys(key):
    single_key = jax.random.fold_in(key, 0)
    gathered_key_rows = jnp.clip(jax.random.normal(single_key, (REQUEST_COUNT, QUERY_TOKENS, KEY_VALUE_HEADS * HEAD_SIZE), jnp.float32), -4.0, 4.0)
    return gathered_key_rows


def draw_new_token_pairs(key, part):
    gathered_key_rows = shared_keys(key)
    key = jax.random.fold_in(key, 3)
    gathered_values = jnp.clip(jax.random.normal(key, (REQUEST_COUNT, QUERY_TOKENS, KEY_VALUE_HEADS * HEAD_SIZE), jnp.float32), -4.0, 4.0)
    return jnp.stack([gathered_key_rows, gathered_values], axis=2).astype(jnp.bfloat16)


def draw_queries(key, part):
    key = jax.random.fold_in(key, 4)
    request_query_rows = jnp.clip(jax.random.normal(key, (REQUEST_COUNT, QUERY_TOKENS, QUERY_HEADS * HEAD_SIZE), jnp.float32), -4.0, 4.0)
    return request_query_rows.astype(jnp.bfloat16)


def draw_page_table(key, part):
    key = jax.random.fold_in(key, 6)
    blocks = REQUEST_COUNT // REQ_DEV
    ranking = jax.random.randint(key, (blocks, PAGES_DEV), 0, 2 ** 20) * PAGES_DEV
    ranking = ranking + jnp.arange(PAGES_DEV, dtype=jnp.int32)[None, :]
    order = jnp.argsort(ranking, axis=1, stable=True).astype(jnp.int32)
    return order.reshape(REQUEST_COUNT, MAXPAGES)


def draw_cache_lengths(key, part):
    key = jax.random.fold_in(key, 7)
    single_key, key_two, key_three = jax.random.split(key, 3)
    shifts = jax.random.randint(single_key, (REQUEST_COUNT,), 0, 6)
    ceiling = jnp.right_shift(jnp.full((REQUEST_COUNT,), MAXLEN, jnp.int32), shifts)
    lengths = jax.random.randint(key_two, (REQUEST_COUNT,), 1, ceiling + 1)
    longest = jax.random.randint(key_three, (), 0, REQUEST_COUNT)
    return lengths.at[longest].set(MAXLEN).astype(jnp.int32)


def draw_residual(key, part):
    key = jax.random.fold_in(key, 8)
    single_key, key_two, key_three = jax.random.split(key, 3)
    base = jnp.clip(jax.random.normal(single_key, (ROWS, D), jnp.float32), -4.0, 4.0)
    limit = 1.15
    row_scale = jnp.exp(jax.random.uniform(key_two, (ROWS, 1), jnp.float32, -limit, limit))
    rising = 0.6 + 1.2 * jnp.arange(D, dtype=jnp.float32)[None, :] / D
    col_scale = jnp.exp(jax.random.uniform(key_three, (1, D), jnp.float32, -limit, limit)) * rising
    return (0.4 * base * row_scale * col_scale).astype(jnp.bfloat16)


def spiked(result, stream_key, source, target, blocks, factor):
    owner, partner = [(jnp.arange(result.shape[axis_at]) // (result.shape[axis_at] // blocks)).reshape([-1 if axis == axis_at else 1 for axis in range(result.ndim)]) for axis_at in (source, target)]
    chosen = jax.random.permutation(stream_key, blocks)[partner]
    strong = (owner == chosen) | (owner == (partner + blocks // 2) % blocks)
    return jnp.where(strong, factor * result, result)


def level_of(own_key, extent, cuts, low, largest):
    def one(dim, shards_of):
        draws = jax.random.uniform(jax.random.fold_in(jax.random.fold_in(own_key, 6), dim), (shards_of,), jnp.float32, low / len(cuts), largest / len(cuts))
        return jnp.repeat(jnp.exp(draws), extent[dim] // shards_of).reshape((-1,) + (1,) * (len(extent) - dim - 1))

    loudness = one(*cuts[0])
    for cut in cuts[1:]:
        loudness = loudness * one(*cut)
    return loudness


def noise(stream_key, extent, width, reach, shards=(), kind=jnp.bfloat16):
    values = width * jax.random.normal(stream_key, extent, jnp.float32)
    if shards:
        values = values * level_of(stream_key, extent, shards, -0.22, 0.18)
    return jnp.clip(values, -reach, reach).astype(kind)


def gaussian_with(own_key, shape, spread, most, cuts, heavy, kind=jnp.bfloat16):
    values = spread * jax.random.normal(own_key, shape, jnp.float32)
    if cuts:
        values = values * level_of(own_key, shape, cuts, -0.22, 0.18)
    return jnp.clip(spiked(values, jax.random.fold_in(own_key, 3), *heavy), -most, most).astype(kind)


def setup_inputs(seed: int = 0) -> dict:
    keys = jax.random.split(jax.random.key(seed), 12)
    queries = draw_queries(jax.random.fold_in(keys[11], 71), 0)
    new_token_pairs = draw_new_token_pairs(jax.random.fold_in(keys[11], 71), 0)
    paged_cache_store = noise(keys[2], (POOL_PAGES, PAGE_TOKENS, 2, KEY_VALUE_HEADS * HEAD_SIZE), 1.0, 5.0, ((0, 64), (3, 2)))
    page_table = draw_page_table(jax.random.fold_in(keys[11], 71), 0)
    cache_lengths = draw_cache_lengths(jax.random.fold_in(keys[11], 71), 0)
    out_weight = noise(keys[5], (QUERY_HEADS * HEAD_SIZE, D), HEAD_SIZE ** -0.5, 0.5, ((0, 2), (1, 64)))
    residual = draw_residual(jax.random.fold_in(keys[11], 71), 0)
    norm_gain = jnp.clip(1.0 + 0.1 * jax.random.normal(keys[7], (D,), jnp.float32), 0.5, 1.5)
    gate_weight = noise(keys[8], (FF, D), D ** -0.5, 0.0625, ((0, 128),))
    up_weight = noise(keys[9], (FF, D), D ** -0.5, 0.0625, ((0, 128),))
    down_weight = gaussian_with(keys[10], (FF, D), FF ** -0.5, 0.125, ((0, 128),), (0, 1, 128, 5.5))
    return {"queries": queries, "new_token_pairs": new_token_pairs, "paged_cache_store": paged_cache_store, "page_table": page_table, "cache_lengths": cache_lengths, "out_weight": out_weight, "residual": residual, "norm_gain": norm_gain, "gate_weight": gate_weight, "up_weight": up_weight, "down_weight": down_weight}


EPS = 1e-05

def reference(queries, new_token_pairs, paged_cache_store, page_table, cache_lengths, out_weight, residual, norm_gain, gate_weight, up_weight, down_weight):
    query_group_width = QUERY_HEADS // KEY_VALUE_HEADS
    cache_span_length = MAXPAGES * PAGE_TOKENS
    factor = 1.0 / HEAD_SIZE ** 0.5
    positions = jnp.arange(cache_span_length, dtype=jnp.int32)
    causal = jnp.arange(QUERY_TOKENS, dtype=jnp.int32)[:, None] >= jnp.arange(QUERY_TOKENS, dtype=jnp.int32)[None, :]

    def attend_one(request_index):
        page_base = request_index // REQ_DEV * PAGES_DEV
        request_page_index = (page_base + page_table[request_index]).astype(jnp.int32)
        cached_pairs = paged_cache_store[request_page_index].reshape(cache_span_length, 2, KEY_VALUE_HEADS, HEAD_SIZE).astype(jnp.float32)
        request_query_rows = queries[request_index].reshape(QUERY_TOKENS, KEY_VALUE_HEADS, query_group_width, HEAD_SIZE).astype(jnp.float32)
        fresh_key_value = new_token_pairs[request_index].reshape(QUERY_TOKENS, 2, KEY_VALUE_HEADS, HEAD_SIZE).astype(jnp.float32)
        cache_scores = jnp.einsum('qkgd,pkd->kgqp', request_query_rows, cached_pairs[:, 0]) * factor
        cache_scores = jnp.where(positions < cache_lengths[request_index], cache_scores, -jnp.inf)
        new_scores = jnp.einsum('qkgd,jkd->kgqj', request_query_rows, fresh_key_value[:, 0]) * factor
        new_scores = jnp.where(causal, new_scores, -jnp.inf)
        peak_score = jnp.maximum(lax.optimization_barrier(jnp.max(cache_scores, axis=-1)), lax.optimization_barrier(jnp.max(new_scores, axis=-1)))
        cache_weights = jnp.exp(cache_scores - peak_score[..., None])
        new_weights = jnp.exp(new_scores - peak_score[..., None])
        weight_sum = lax.optimization_barrier(jnp.sum(cache_weights, axis=-1)) + lax.optimization_barrier(jnp.sum(new_weights, axis=-1))
        cache_probs = lax.optimization_barrier(cache_weights.astype(jnp.bfloat16)).astype(jnp.float32)
        new_probs = lax.optimization_barrier(new_weights.astype(jnp.bfloat16)).astype(jnp.float32)
        numerator = jnp.einsum('kgqp,pkd->qkgd', cache_probs, cached_pairs[:, 1])
        numerator = numerator + jnp.einsum('kgqj,jkd->qkgd', new_probs, fresh_key_value[:, 1])
        output = numerator / weight_sum.transpose(2, 0, 1)[..., None]
        return output.reshape(QUERY_TOKENS, QUERY_HEADS * HEAD_SIZE).astype(jnp.bfloat16)
    attn_out = lax.map(attend_one, jnp.arange(REQUEST_COUNT, dtype=jnp.int32))
    attn_rows = attn_out.reshape(ROWS, QUERY_HEADS * HEAD_SIZE)
    mixed = jnp.dot(attn_rows, out_weight, preferred_element_type=jnp.float32)
    stream = (residual.astype(jnp.float32) + mixed).astype(jnp.bfloat16)
    stream_wide = stream.astype(jnp.float32)
    inv_rms = lax.rsqrt(lax.optimization_barrier(jnp.mean(stream_wide * stream_wide, axis=1, keepdims=True)) + EPS)
    normed = (stream_wide * inv_rms * norm_gain[None, :]).astype(jnp.bfloat16)
    gate_proj = jnp.dot(normed, gate_weight.T, preferred_element_type=jnp.float32)
    up_proj = jnp.dot(normed, up_weight.T, preferred_element_type=jnp.float32)
    hidden = (jax.nn.silu(gate_proj) * up_proj).astype(jnp.bfloat16)
    ffn_sum = jnp.dot(hidden, down_weight, preferred_element_type=jnp.float32)
    return (stream_wide + ffn_sum).astype(jnp.bfloat16)
```

```python
import functools
import math

import jax
import jax.numpy as jnp
from jax import lax
from jax.experimental import pallas as pl
from jax.experimental.pallas import tpu as pltpu
from jax.sharding import PartitionSpec as P

D = 8192
HEAD_SIZE = 128
EPS = 1e-05
MESH = pl.DeviceIdType.MESH
F32 = jnp.float32
BF16 = jnp.bfloat16

PAGE = 64
CHUNK_PAGES = 4
CHUNK = PAGE * CHUNK_PAGES
MAXLEN = 3072
NEW_ROWS = 64
REQS = 2
KV_HEADS = 4
GROUP = 8
TOKENS = 4

PARTS = ((0, 80), (80, 80), (160, 96))
ORDERS = (("x", "y", "z"), ("y", "z", "x"), ("z", "x", "y"))
LAYOUT = ("z", "y", "x")


def attend(table, lengths, q_ref, new_ref, kv_ref, out_ref, buf, s_buf, o32, sems, new_sems):
    flat = buf.reshape(KV_HEADS, REQS, (MAXLEN + NEW_ROWS) * 2, HEAD_SIZE)
    factor = 1.0 / math.sqrt(HEAD_SIZE)

    for r in range(REQS):
        chunks = (lengths[r] + CHUNK - 1) // CHUNK

        def start(p, _, r=r):
            page = table[r, p]
            for h in range(KV_HEADS):
                pltpu.make_async_copy(
                    kv_ref.at[page, :, :, pl.ds(h * HEAD_SIZE, HEAD_SIZE)],
                    buf.at[h, r, pl.ds(p * PAGE, PAGE)],
                    sems.at[r, p // CHUNK_PAGES],
                ).start()
            return 0

        lax.fori_loop(0, chunks * CHUNK_PAGES, start, 0)

    for r in range(REQS):
        for h in range(KV_HEADS):
            flat[h, r, pl.ds(2 * MAXLEN, 2 * NEW_ROWS), :] = jnp.zeros((2 * NEW_ROWS, HEAD_SIZE), BF16)
    new_copies = []
    for r in range(REQS):
        for h in range(KV_HEADS):
            copy = pltpu.make_async_copy(
                new_ref.at[r, :, :, pl.ds(h * HEAD_SIZE, HEAD_SIZE)],
                buf.at[h, r, pl.ds(MAXLEN, TOKENS)],
                new_sems.at[r, h],
            )
            copy.start()
            new_copies.append(copy)

    rows = GROUP * TOKENS
    for copy in new_copies:
        copy.wait()
    for r in range(REQS):
        length = lengths[r]
        chunks = (length + CHUNK - 1) // CHUNK
        wide = q_ref[r].astype(F32)
        q = [
            jnp.concatenate(
                [wide[:, (h * GROUP + g) * HEAD_SIZE : (h * GROUP + g + 1) * HEAD_SIZE] for g in range(GROUP)], axis=0
            ).astype(BF16)
            for h in range(KV_HEADS)
        ]

        col = lax.broadcasted_iota(jnp.int32, (rows, 2 * NEW_ROWS), 1)
        row = lax.broadcasted_iota(jnp.int32, (rows, 2 * NEW_ROWS), 0)
        live = (col % 2 == 0) & (col // 2 <= row % TOKENS)
        fresh = []
        for h in range(KV_HEADS):
            s = lax.dot_general(
                q[h], flat[h, r, pl.ds(2 * MAXLEN, 2 * NEW_ROWS), :], (((1,), (1,)), ((), ())),
                preferred_element_type=F32,
            )
            fresh.append(jnp.where(live, s * factor, -jnp.inf))

        wide_col = lax.broadcasted_iota(jnp.int32, (rows, 2 * CHUNK), 1)

        def score(c, peaks, r=r, q=q, length=length):
            pltpu.make_async_copy(
                buf.at[:, r, pl.ds(c * CHUNK, CHUNK)], buf.at[:, r, pl.ds(c * CHUNK, CHUNK)], sems.at[r, c]
            ).wait()
            keep = (wide_col % 2 == 0) & (wide_col < 2 * (length - c * CHUNK))
            out = []
            for h in range(KV_HEADS):
                s = lax.dot_general(
                    q[h], flat[h, r, pl.ds(pl.multiple_of(c * 2 * CHUNK, 2 * CHUNK), 2 * CHUNK), :],
                    (((1,), (1,)), ((), ())), preferred_element_type=F32,
                )
                s = jnp.where(keep, s * factor, -jnp.inf)
                s_buf[c, h] = s
                m = peaks[h]
                for t in range(2 * CHUNK // 128):
                    m = jnp.maximum(m, s[:, t * 128 : (t + 1) * 128])
                out.append(m)
            return tuple(out)

        peaks = lax.fori_loop(0, chunks, score, tuple(fresh))
        peaks = [jnp.max(m, axis=1, keepdims=True) for m in peaks]

        sums, totals = [], []
        for h in range(KV_HEADS):
            w = jnp.exp(fresh[h] - peaks[h])
            sums.append(w)
            totals.append(
                jnp.dot(
                    pltpu.roll(w, 1, 1).astype(BF16), flat[h, r, pl.ds(2 * MAXLEN, 2 * NEW_ROWS), :],
                    preferred_element_type=F32,
                )
            )

        def weigh(c, carry, r=r, peaks=peaks):
            sums, totals = carry
            new_sums, new_totals = [], []
            for h in range(KV_HEADS):
                total_w = sums[h]
                shifted = []
                for t in range(2 * CHUNK // 128):
                    w = jnp.exp(s_buf[c, h, :, t * 128 : (t + 1) * 128] - peaks[h])
                    total_w = total_w + w
                    shifted.append(pltpu.roll(w, 1, 1).astype(BF16))
                new_sums.append(total_w)
                new_totals.append(
                    totals[h]
                    + jnp.dot(
                        jnp.concatenate(shifted, axis=1),
                        flat[h, r, pl.ds(pl.multiple_of(c * 2 * CHUNK, 2 * CHUNK), 2 * CHUNK), :],
                        preferred_element_type=F32,
                    )
                )
            return tuple(new_sums), tuple(new_totals)

        sums, totals = lax.fori_loop(0, chunks, weigh, (tuple(sums), tuple(totals)))
        for h in range(KV_HEADS):
            out = totals[h] / jnp.sum(sums[h], axis=1, keepdims=True)
            for g in range(GROUP):
                o32[h * GROUP + g, r * TOKENS : (r + 1) * TOKENS, :] = out[g * TOKENS : (g + 1) * TOKENS]
    out_ref[...] = o32[...].reshape(KV_HEADS * GROUP * REQS * TOKENS, HEAD_SIZE).astype(BF16)


def attention(queries, new_token_pairs, paged_cache_store, page_table, cache_lengths):
    smem = pl.BlockSpec(memory_space=pltpu.SMEM)
    vmem = pl.BlockSpec(memory_space=pltpu.VMEM)
    anywhere = pl.BlockSpec(memory_space=pl.ANY)
    return pl.pallas_call(
        attend,
        out_shape=jax.ShapeDtypeStruct((256, HEAD_SIZE), BF16),
        in_specs=[smem, smem, vmem, anywhere, anywhere],
        out_specs=vmem,
        scratch_shapes=[
            pltpu.VMEM((KV_HEADS, REQS, MAXLEN + NEW_ROWS, 2, HEAD_SIZE), BF16),
            pltpu.VMEM((MAXLEN // CHUNK, KV_HEADS, GROUP * TOKENS, 2 * CHUNK), F32),
            pltpu.VMEM((KV_HEADS * GROUP, REQS * TOKENS, HEAD_SIZE), F32),
            pltpu.SemaphoreType.DMA((REQS, MAXLEN // CHUNK)),
            pltpu.SemaphoreType.DMA((REQS, KV_HEADS)),
        ],
        compiler_params=pltpu.CompilerParams(vmem_limit_bytes=58 << 20),
        name="paged_attention",
    )(page_table, cache_lengths, queries, new_token_pairs, paged_cache_store)


def layer(
    attn, residual, gain, w_out, w_gate, w_up, w_down, out_ref,
    A, X, Q, RC, R1, R2, R3, sec_in, sec_out, fin_in, fin_out,
    wo, wg, wu, wd, acc_g, acc_u, acc_s, hidden, mixed_own,
    w_sem, s1, r1, f1s, f1r, s2, r2, f2s, f2r, cs, cr, s3, r3, xs, xr,
):
    sec = lax.axis_index("sec")
    grp = lax.axis_index("grp")
    tp = lax.axis_index("tp")
    zh, c = grp // 2, grp % 2
    me = {"z": zh * 2 + sec, "y": tp // 4, "x": tp % 4}

    def device(at, core):
        return (at["z"] % 2, (at["z"] // 2) * 2 + core, at["y"] * 4 + at["x"])

    def shifted(axis, k):
        return {**me, axis: (me[axis] + k) % 4}

    sibling = device(me, 1 - c)
    partner = device({**me, "z": zh * 2 + (1 - sec)}, c)

    def weight_copy(i, src, dst):
        return pltpu.make_async_copy(src, dst, w_sem.at[i])

    loads = [
        weight_copy(0, w_out, wo), weight_copy(1, w_gate, wg), weight_copy(2, w_up, wu), weight_copy(3, w_down, wd)
    ]
    for load in loads:
        load.start()

    barrier = pltpu.get_barrier_semaphore()
    for axis in LAYOUT:
        for k in (1, 2, 3):
            pl.semaphore_signal(barrier, 1, device_id=device(shifted(axis, k), c), device_id_type=MESH)
    pl.semaphore_signal(barrier, 1, device_id=sibling, device_id_type=MESH)
    pl.semaphore_wait(barrier, 10)

    def remote(src, dst, send, recv, to):
        return pltpu.make_async_remote_copy(src, dst, send, recv, device_id=to, device_id_type=MESH)

    def gather(buf, coord, offsets, send, recv, fsend, frecv, between):
        def region(at, rows):
            return buf.at[at["z"], c, at["y"], at["x"], pl.ds(*rows)]

        forwards = []

        def forward(at, rows, slot):
            part = region(at, rows)
            copy = remote(part, part, fsend.at[slot], frecv.at[slot], sibling)
            copy.start()
            forwards.append(copy)

        forward(coord, (0, 256), 27)
        held = [dict(coord) for _ in PARTS]
        flying = []

        def launch(p, stage):
            axis = ORDERS[p][stage]
            for k in offsets[axis]:
                slot = p * 9 + stage * 3 + k - 1
                block = region(held[p], PARTS[p])
                copy = remote(block, block, send.at[slot], recv.at[slot], device(shifted(axis, k), c))
                copy.start()
                flying.append(copy)
                pending[p].append((copy, slot, axis, k))

        pending = [[] for _ in PARTS]
        for p in range(3):
            launch(p, 0)
        between()
        for stage in range(3):
            for p in range(3):
                arrived = pending[p]
                pending[p] = []
                for copy, slot, axis, k in arrived:
                    copy.wait_recv()
                axis = ORDERS[p][stage]
                landed = [
                    ({**held[p], axis: (coord[axis] - (k if len(offsets[axis]) == 3 else 1)) % (4 if len(offsets[axis]) == 3 else 2)}, slot)
                    for _, slot, _, k in arrived
                ]
                held[p] = {**held[p], axis: slice(None)}
                if stage < 2:
                    launch(p, stage + 1)
                for at, slot in landed:
                    forward(at, PARTS[p], slot)
        for copy in flying:
            copy.wait_send()
        for copy in forwards:
            copy.wait()

    def scale_weights():
        loads[1].wait()
        loads[2].wait()

        def scale(i, _):
            cols = pl.ds(pl.multiple_of(i * 256, 256), 256)
            g = gain[:, cols]
            wg[:, cols] = (wg[:, cols].astype(F32) * g).astype(BF16)
            wu[:, cols] = (wu[:, cols].astype(F32) * g).astype(BF16)
            return 0

        lax.fori_loop(0, D // 256, scale, 0)

    A[zh, c, me["y"], me["x"]] = attn[...]
    gather(
        A, {"z": zh, "y": me["y"], "x": me["x"]}, {"z": (2,), "y": (1, 2, 3), "x": (1, 2, 3)},
        s1, r1, f1s, f1r, scale_weights,
    )

    loads[0].wait()

    def project(half):
        total = jnp.zeros((512, 256), F32)
        for j in range(0, 16, 2):
            lhs = jnp.concatenate(
                [A[half, :, :, :, (j + t) * 16 : (j + t + 1) * 16, :].reshape(512, 128) for t in range(2)], axis=1
            )
            rhs = jnp.concatenate(
                [
                    jnp.concatenate(
                        [wo[(2 * (j + t) + u) * 128 : (2 * (j + t) + u + 1) * 128, :] for u in range(2)], axis=1
                    )
                    for t in range(2)
                ],
                axis=0,
            )
            total = total + jnp.dot(lhs, rhs, preferred_element_type=F32)
        total = total.reshape(32, 2, 8, 256)
        return (total[:, 0, :, :128] + total[:, 1, :, 128:]).reshape(256, 128)

    sec_out[...] = project(1 - sec).astype(BF16)
    swap = remote(sec_out, sec_in, xs.at[0], xr.at[0], partner)
    swap.start()
    mixed_own[...] = project(sec)
    swap.wait()
    half_rows = pl.ds(pl.multiple_of(sec * 256, 256), 256)
    stream = (residual[half_rows, :].astype(F32) + (mixed_own[...] + sec_in[...].astype(F32))).astype(BF16)
    X[me["z"], c, me["y"], me["x"]] = stream

    gather(
        X, me, {"z": (1, 2, 3), "y": (1, 2, 3), "x": (1, 2, 3)}, s2, r2, f2s, f2r, lambda: None
    )

    acc_g[...] = jnp.zeros_like(acc_g)
    acc_u[...] = jnp.zeros_like(acc_u)
    acc_s[...] = jnp.zeros_like(acc_s)

    def ffn_in(i, _):
        hi, core, y0 = i // 4, (i // 2) % 2, (i % 2) * 2
        cols = pl.ds(pl.multiple_of(i * 1024, 1024), 1024)
        halves = []
        for lo in range(2):
            blocks = [X[hi * 2 + lo, core, y0 + b // 4, b % 4] for b in range(8)]
            squares = acc_s[lo * 256 : (lo + 1) * 256]
            for b in blocks:
                wide = b.astype(F32)
                squares = squares + wide * wide
            acc_s[lo * 256 : (lo + 1) * 256] = squares
            halves.append(jnp.concatenate(blocks, axis=1))
        lhs = jnp.concatenate(halves, axis=0)
        nt = (((1,), (1,)), ((), ()))
        acc_g[...] += lax.dot_general(lhs, wg[:, cols], nt, preferred_element_type=F32)
        acc_u[...] += lax.dot_general(lhs, wu[:, cols], nt, preferred_element_type=F32)
        return 0

    lax.fori_loop(0, 8, ffn_in, 0)
    inv = lax.rsqrt(jnp.sum(acc_s[...], axis=1, keepdims=True) / D + EPS)
    gate = acc_g[...] * inv
    hidden[...] = (gate / (1.0 + jnp.exp(-gate)) * (acc_u[...] * inv)).astype(BF16)

    loads[3].wait()

    def ffn_out(core, hi, y):
        cols = pl.ds(pl.multiple_of(((hi * 2 + core) * 16 + y * 4) * 128, 512), 512)
        part = jnp.dot(hidden[...], wd[:, cols], preferred_element_type=F32).astype(BF16)
        for lo in range(2):
            for x in range(4):
                Q[hi * 2 + lo, core, y, x] = part[lo * 256 : (lo + 1) * 256, x * 128 : (x + 1) * 128]

    def core_copy(i):
        hi, y = i // 4, i % 4
        return remote(
            Q.at[pl.ds(hi * 2, 2), 1 - c, y], RC.at[pl.ds(hi * 2, 2), y], cs.at[i], cr.at[i], sibling
        )

    def to_sibling(i, _):
        ffn_out(1 - c, i // 4, i % 4)
        core_copy(i).start()
        return 0

    def own(i, _):
        ffn_out(c, i // 4, i % 4)
        return 0

    lax.fori_loop(0, 8, to_sibling, 0)
    lax.fori_loop(0, 8, own, 0)

    def add_sibling(i, _):
        hi, y = i // 4, i % 4
        core_copy(i).wait_recv()
        for lo in range(2):
            z = hi * 2 + lo
            for x in range(4):
                Q[z, c, y, x] = (Q[z, c, y, x].astype(F32) + RC[z, y, x].astype(F32)).astype(BF16)
        return 0

    lax.fori_loop(0, 8, add_sibling, 0)

    flying = []

    def launch_sum(p, stage):
        order = ORDERS[p][::-1]
        axis, left = order[stage], order[stage + 1 :]
        rows = pl.ds(*PARTS[p])
        for k in (1, 2, 3):
            slot = p * 9 + stage * 3 + k - 1
            at = {a: (slice(None) if a in left else me[a]) for a in LAYOUT}
            at[axis] = (me[axis] + k) % 4
            src = Q.at[at["z"], c, at["y"], at["x"], rows]
            dst = (R1.at[k - 1, :, :, rows], R2.at[k - 1, :, rows], R3.at[k - 1, rows])[stage]
            copy = remote(src, dst, s3.at[slot], r3.at[slot], device(shifted(axis, k), c))
            copy.start()
            flying.append(copy)
            arriving[p].append(copy)

    def add_sum(p, stage):
        order = ORDERS[p][::-1]
        left = [a for a in LAYOUT if a in order[stage + 1 :]]
        rows = pl.ds(*PARTS[p])
        for copy in arriving[p]:
            copy.wait_recv()
        arriving[p] = []
        if stage == 2:
            return

        def add(i, _):
            where = (i // 4, i % 4) if stage == 0 else (i,)
            at = {**me, **dict(zip(left, where))}
            total = Q[at["z"], c, at["y"], at["x"], rows].astype(F32)
            for k in range(3):
                got = R1[k, where[0], where[1], rows] if stage == 0 else R2[k, where[0], rows]
                total = total + got.astype(F32)
            Q[at["z"], c, at["y"], at["x"], rows] = total.astype(BF16)
            return 0

        lax.fori_loop(0, 16 if stage == 0 else 4, add, 0)

    arriving = [[] for _ in PARTS]
    for p in range(3):
        launch_sum(p, 0)
    for stage in range(3):
        for p in range(3):
            add_sum(p, stage)
            if stage < 2:
                launch_sum(p, stage + 1)

    total = X[me["z"], c, me["y"], me["x"]].astype(F32)
    ffn = Q[me["z"], c, me["y"], me["x"]].astype(F32)
    for k in range(3):
        ffn = ffn + R3[k].astype(F32)
    done = (total + ffn).astype(BF16)
    fin_out[...] = done
    last = remote(fin_out, fin_in, xs.at[1], xr.at[1], partner)
    last.start()
    out_ref[half_rows, :] = done

    def sent(i, _):
        core_copy(i).wait_send()
        return 0

    lax.fori_loop(0, 8, sent, 0)
    for copy in flying:
        copy.wait_send()
    last.wait()
    out_ref[pl.ds(pl.multiple_of((1 - sec) * 256, 256), 256), :] = fin_in[...]


def rest(attn, residual, gain, w_out, w_gate, w_up, w_down):
    vmem = pl.BlockSpec(memory_space=pltpu.VMEM)
    anywhere = pl.BlockSpec(memory_space=pl.ANY)
    dma = pltpu.SemaphoreType.DMA
    return pl.pallas_call(
        layer,
        out_shape=jax.ShapeDtypeStruct((512, 128), BF16),
        in_specs=[vmem, vmem, vmem, anywhere, anywhere, anywhere, anywhere],
        out_specs=vmem,
        scratch_shapes=[
            pltpu.VMEM((2, 2, 4, 4, 256, 128), BF16),
            pltpu.VMEM((4, 2, 4, 4, 256, 128), BF16),
            pltpu.VMEM((4, 2, 4, 4, 256, 128), BF16),
            pltpu.VMEM((4, 4, 4, 256, 128), BF16),
            pltpu.VMEM((3, 4, 4, 256, 128), BF16),
            pltpu.VMEM((3, 4, 256, 128), BF16),
            pltpu.VMEM((3, 256, 128), BF16),
            pltpu.VMEM((256, 128), BF16),
            pltpu.VMEM((256, 128), BF16),
            pltpu.VMEM((256, 128), BF16),
            pltpu.VMEM((256, 128), BF16),
            pltpu.VMEM(w_out.shape, BF16),
            pltpu.VMEM(w_gate.shape, BF16),
            pltpu.VMEM(w_up.shape, BF16),
            pltpu.VMEM(w_down.shape, BF16),
            pltpu.VMEM((512, w_gate.shape[0]), F32),
            pltpu.VMEM((512, w_gate.shape[0]), F32),
            pltpu.VMEM((512, 128), F32),
            pltpu.VMEM((512, w_gate.shape[0]), BF16),
            pltpu.VMEM((256, 128), F32),
            dma((4,)),
            dma((27,)), dma((27,)), dma((28,)), dma((28,)),
            dma((27,)), dma((27,)), dma((28,)), dma((28,)),
            dma((8,)), dma((8,)),
            dma((27,)), dma((27,)),
            dma((2,)), dma((2,)),
        ],
        compiler_params=pltpu.CompilerParams(collective_id=0, has_side_effects=True, vmem_limit_bytes=60 << 20),
        name="layer_rest",
    )(attn, residual, gain, w_out, w_gate, w_up, w_down)


def per_device(
    queries, new_token_pairs, paged_cache_store, page_table, cache_lengths,
    out_weight, residual, norm_gain, gate_weight, up_weight, down_weight,
):
    attn = attention(queries, new_token_pairs, paged_cache_store, page_table, cache_lengths)
    return rest(attn, residual, norm_gain.reshape(1, D), out_weight, gate_weight, up_weight, down_weight)


def solution(mesh):
    in_specs = (
        P(("grp", "tp"), None, "sec"),
        P(("grp", "tp"), None, None, "sec"),
        P(("grp", "tp"), None, None, "sec"),
        P(("grp", "tp"), None),
        P(("grp", "tp")),
        P("sec", ("grp", "tp")),
        P(None, ("grp", "tp")),
        P(),
        P(("sec", "grp", "tp"), None),
        P(("sec", "grp", "tp"), None),
        P(("sec", "grp", "tp"), None),
    )
    out_specs = P(None, ("grp", "tp"))
    return jax.shard_map(
        per_device, mesh=mesh, in_specs=in_specs, out_specs=out_specs, check_vma=False
    )
```

```python
import functools
import math

import jax
import jax.numpy as jnp
from jax import lax
from jax.experimental import pallas as pl
from jax.experimental.pallas import tpu as pltpu
from jax.sharding import PartitionSpec as P

D = 8192
HEAD_SIZE = 128
EPS = 1e-05
MESH = pl.DeviceIdType.MESH
F32 = jnp.float32
BF16 = jnp.bfloat16

PAGE = 64
CHUNK_PAGES = 8
CHUNK = PAGE * CHUNK_PAGES
MAXLEN = 3072
REQS = 2
KV_HEADS = 4
GROUP = 8
TOKENS = 4
NEW_ROWS = REQS * TOKENS * 2

PARTS = ((0, 80), (80, 80), (160, 96))
HALF_PARTS = (((0, 48), (48, 48), (96, 32)), ((128, 32), (160, 48), (208, 48)))
HALF = 128
ORDERS = (("x", "y", "z"), ("y", "z", "x"), ("z", "x", "y"))
LAYOUT = ("z", "y", "x")


def attend(table, lengths, q_ref, new_ref, kv_ref, out_ref, flat, new_flat, s_buf, acc, o32, sems, new_sems):
    kv_rows = kv_ref.reshape(kv_ref.shape[0], 2 * PAGE, KV_HEADS * HEAD_SIZE)
    new_rows = new_ref.reshape(NEW_ROWS, KV_HEADS * HEAD_SIZE)
    factor = 1.0 / math.sqrt(HEAD_SIZE)
    rows = GROUP * TOKENS
    queries = KV_HEADS * rows
    nt = (((1,), (1,)), ((), ()))

    new_copies = []
    new_flat[:, pl.ds(NEW_ROWS, 128 - NEW_ROWS), :] = jnp.zeros((KV_HEADS, 128 - NEW_ROWS, HEAD_SIZE), BF16)
    for h in range(KV_HEADS):
        copy = pltpu.make_async_copy(
            new_rows.at[:, pl.ds(h * HEAD_SIZE, HEAD_SIZE)], new_flat.at[h, pl.ds(0, NEW_ROWS)], new_sems.at[h]
        )
        copy.start()
        new_copies.append(copy)

    for r in range(REQS):
        chunks = (lengths[r] + CHUNK - 1) // CHUNK

        def start(p, _, r=r):
            page = table[r, p]
            for h in range(KV_HEADS):
                pltpu.make_async_copy(
                    kv_rows.at[page, :, pl.ds(h * HEAD_SIZE, HEAD_SIZE)],
                    flat.at[h, r, pl.ds(pl.multiple_of(p * 2 * PAGE, 2 * PAGE), 2 * PAGE)],
                    sems.at[r, p // CHUNK_PAGES],
                ).start()
            return 0

        lax.fori_loop(0, chunks * CHUNK_PAGES, start, 0)

    stacked = []
    for r in range(REQS):
        wide = q_ref[r].astype(F32)
        blocks = []
        for h in range(KV_HEADS):
            q = jnp.concatenate(
                [wide[:, (h * GROUP + g) * HEAD_SIZE : (h * GROUP + g + 1) * HEAD_SIZE] for g in range(GROUP)], axis=0
            ).astype(BF16)
            zero = jnp.zeros_like(q)
            blocks.append(jnp.concatenate([q if k == h else zero for k in range(KV_HEADS)], axis=1))
        stacked.append(jnp.concatenate(blocks, axis=0))

    def pairs(r, first, count):
        return jnp.concatenate([flat[h, r, pl.ds(first, count), :] for h in range(KV_HEADS)], axis=1)

    col = lax.broadcasted_iota(jnp.int32, (queries, 128), 1)
    row = lax.broadcasted_iota(jnp.int32, (queries, 128), 0)
    wide_col = lax.broadcasted_iota(jnp.int32, (8, 2 * CHUNK), 1)
    place = jnp.where(wide_col % 2 == 0, wide_col, 2 * MAXLEN)[:1]

    for copy in new_copies:
        copy.wait()
    new_pairs = jnp.concatenate([new_flat[h] for h in range(KV_HEADS)], axis=1)
    fresh = []
    for r in range(REQS):
        s = lax.dot_general(stacked[r], new_pairs, nt, preferred_element_type=F32)
        token = (col - r * 2 * TOKENS) // 2
        live = (col % 2 == 0) & (col >= r * 2 * TOKENS) & (token <= row % TOKENS)
        fresh.append(jnp.where(live, s * factor, -jnp.inf))

    for r in range(REQS):
        length = lengths[r]
        chunks = (length + CHUNK - 1) // CHUNK
        q = stacked[r]

        def score(c, peak, r=r, q=q, length=length):
            here = flat.at[:, r, pl.ds(pl.multiple_of(c * 2 * CHUNK, 2 * CHUNK), 2 * CHUNK)]
            pltpu.make_async_copy(
                here, here, sems.at[r, c]
            ).wait()
            s = lax.dot_general(
                q, pairs(r, pl.multiple_of(c * 2 * CHUNK, 2 * CHUNK), 2 * CHUNK), nt, preferred_element_type=F32
            )
            s = jnp.where(place < 2 * (length - c * CHUNK), s * factor, -jnp.inf)
            s_buf[c] = s
            for t in range(2 * CHUNK // 128):
                peak = jnp.maximum(peak, s[:, t * 128 : (t + 1) * 128])
            return peak

        peak = jnp.max(lax.fori_loop(0, chunks, score, fresh[r]), axis=1, keepdims=True)

        w = jnp.exp(fresh[r] - peak)
        acc[...] = jnp.dot(
            pltpu.roll(w, 1, 1).astype(BF16), new_pairs, preferred_element_type=F32
        )

        def weigh(c, total, r=r, peak=peak):
            moved = []
            for t in range(2 * CHUNK // 128):
                w = jnp.exp(s_buf[c, :, t * 128 : (t + 1) * 128] - peak)
                total = total + w
                moved.append(pltpu.roll(w, 1, 1).astype(BF16))
            acc[...] += jnp.dot(
                jnp.concatenate(moved, axis=1),
                pairs(r, pl.multiple_of(c * 2 * CHUNK, 2 * CHUNK), 2 * CHUNK),
                preferred_element_type=F32,
            )
            return total

        total = jnp.sum(lax.fori_loop(0, chunks, weigh, w), axis=1, keepdims=True)
        for h in range(KV_HEADS):
            here = slice(h * rows, (h + 1) * rows)
            out = acc[here, h * HEAD_SIZE : (h + 1) * HEAD_SIZE] / total[here]
            for g in range(GROUP):
                o32[h * GROUP + g, r * TOKENS : (r + 1) * TOKENS, :] = out[g * TOKENS : (g + 1) * TOKENS]
    out_ref[...] = o32[...].reshape(KV_HEADS * GROUP * REQS * TOKENS, HEAD_SIZE).astype(BF16)


def attention(queries, new_token_pairs, paged_cache_store, page_table, cache_lengths):
    smem = pl.BlockSpec(memory_space=pltpu.SMEM)
    vmem = pl.BlockSpec(memory_space=pltpu.VMEM)
    anywhere = pl.BlockSpec(memory_space=pl.ANY)
    return pl.pallas_call(
        attend,
        out_shape=jax.ShapeDtypeStruct((256, HEAD_SIZE), BF16),
        in_specs=[smem, smem, vmem, anywhere, anywhere],
        out_specs=vmem,
        scratch_shapes=[
            pltpu.VMEM((KV_HEADS, REQS, 2 * MAXLEN, HEAD_SIZE), BF16),
            pltpu.VMEM((KV_HEADS, 128, HEAD_SIZE), BF16),
            pltpu.VMEM((MAXLEN // CHUNK, KV_HEADS * GROUP * TOKENS, 2 * CHUNK), F32),
            pltpu.VMEM((KV_HEADS * GROUP * TOKENS, KV_HEADS * HEAD_SIZE), F32),
            pltpu.VMEM((KV_HEADS * GROUP, REQS * TOKENS, HEAD_SIZE), F32),
            pltpu.SemaphoreType.DMA((REQS, MAXLEN // CHUNK)),
            pltpu.SemaphoreType.DMA((KV_HEADS,)),
        ],
        compiler_params=pltpu.CompilerParams(vmem_limit_bytes=58 << 20),
        name="paged_attention",
    )(page_table, cache_lengths, queries, new_token_pairs, paged_cache_store)


class Gather:
    def __init__(self, net, buf, coord, offsets, parts, rows, sems, base):
        self.net, self.buf, self.coord, self.offsets, self.parts, self.rows = net, buf, coord, offsets, parts, rows
        self.send, self.recv, self.fsend, self.frecv = sems
        self.base, self.fbase = base * 27, base * 28
        self.held = [dict(coord) for _ in parts]
        self.pending = [[] for _ in parts]
        self.flying, self.forwards = [], []

    def region(self, at, rows):
        return self.buf.at[at["z"], self.net.core, at["y"], at["x"], pl.ds(*rows)]

    def forward(self, at, rows, slot):
        part = self.region(at, rows)
        slot = self.fbase + slot
        copy = self.net.copy(part, part, self.fsend.at[slot], self.frecv.at[slot], self.net.sibling)
        copy.start()
        self.forwards.append(copy)

    def launch(self, p, stage):
        axis = ORDERS[p][stage]
        for k in self.offsets[axis]:
            slot = p * 9 + stage * 3 + k - 1
            block = self.region(self.held[p], self.parts[p])
            copy = self.net.copy(
                block, block, self.send.at[self.base + slot], self.recv.at[self.base + slot], self.net.shifted(axis, k)
            )
            copy.start()
            self.flying.append(copy)
            self.pending[p].append((copy, slot, k))

    def start(self):
        for p in range(3):
            self.launch(p, 0)
        self.forward(self.coord, self.rows, 27)

    def step(self, stage):
        for p in range(3):
            axis = ORDERS[p][stage]
            full = len(self.offsets[axis]) == 3
            arrived, self.pending[p] = self.pending[p], []
            landed = []
            for copy, slot, k in arrived:
                copy.wait_recv()
                came = (self.coord[axis] + 4 - k) % 4 if full else 1 - self.coord[axis]
                landed.append(({**self.held[p], axis: came}, slot))
            self.held[p] = {**self.held[p], axis: slice(None)}
            if stage < 2:
                self.launch(p, stage + 1)
            for at, slot in landed:
                self.forward(at, self.parts[p], slot)

    def finish(self):
        for copy in self.forwards:
            copy.wait_recv()

    def drain(self):
        for copy in self.flying + self.forwards:
            copy.wait_send()


class Scatter:
    def __init__(self, net, Q, landing, parts, sems, base):
        self.net, self.Q, self.landing, self.parts = net, Q, landing, parts
        self.send, self.recv = sems
        self.base = base * 27
        self.pending = [[] for _ in parts]
        self.flying = []

    def launch(self, p, stage):
        order = ORDERS[p][::-1]
        axis, left = order[stage], order[stage + 1 :]
        rows = pl.ds(*self.parts[p])
        me = self.net.me
        for k in (1, 2, 3):
            slot = self.base + p * 9 + stage * 3 + k - 1
            at = {a: (slice(None) if a in left else me[a]) for a in LAYOUT}
            at[axis] = (me[axis] + k) % 4
            src = self.Q.at[at["z"], self.net.core, at["y"], at["x"], rows]
            dst = self.landing[stage].at[(k - 1, *(slice(None),) * len(left), rows)]
            copy = self.net.copy(src, dst, self.send.at[slot], self.recv.at[slot], self.net.shifted(axis, k))
            copy.start()
            self.flying.append(copy)
            self.pending[p].append(copy)

    def start(self):
        for p in range(3):
            self.launch(p, 0)

    def step(self, stage):
        for p in range(3):
            order = ORDERS[p][::-1]
            left = [a for a in LAYOUT if a in order[stage + 1 :]]
            rows = pl.ds(*self.parts[p])
            me, core, Q = self.net.me, self.net.core, self.Q
            land = self.landing[stage]
            for copy in self.pending[p]:
                copy.wait_recv()
            self.pending[p] = []
            if stage == 2:
                continue

            def add(i, _, left=left, rows=rows, land=land):
                where = (i // 4, i % 4) if stage == 0 else (i,)
                at = {**me, **dict(zip(left, where))}
                total = Q[at["z"], core, at["y"], at["x"], rows].astype(F32)
                for k in range(3):
                    got = land[k, where[0], where[1], rows] if stage == 0 else land[k, where[0], rows]
                    total = total + got.astype(F32)
                Q[at["z"], core, at["y"], at["x"], rows] = total.astype(BF16)
                return 0

            lax.fori_loop(0, 16 if stage == 0 else 4, add, 0)
            self.launch(p, stage + 1)

    def drain(self):
        for copy in self.flying:
            copy.wait_send()


class Net:
    def __init__(self):
        sec, grp, tp = lax.axis_index("sec"), lax.axis_index("grp"), lax.axis_index("tp")
        self.sec, self.zh, self.core = sec, grp // 2, grp % 2
        self.me = {"z": self.zh * 2 + sec, "y": tp // 4, "x": tp % 4}
        self.sibling = self.device(self.me, 1 - self.core)
        self.partner = self.device({**self.me, "z": self.zh * 2 + (1 - sec)}, self.core)

    def device(self, at, core):
        return (at["z"] % 2, (at["z"] // 2) * 2 + core, at["y"] * 4 + at["x"])

    def shifted(self, axis, k):
        return self.device({**self.me, axis: (self.me[axis] + k) % 4}, self.core)

    def copy(self, src, dst, send, recv, to):
        return pltpu.make_async_remote_copy(src, dst, send, recv, device_id=to, device_id_type=MESH)


def layer(
    attn, residual, gain, w_out, w_gate, w_up, w_down, out_ref,
    A, X, Q, RC, R1, R2, R3, sec_in, sec_out, fin_in, fin_out,
    wo, wg, wu, wd, acc_g, acc_u, acc_s, hidden, mixed,
    w_sem, s1, r1, f1s, f1r, s2, r2, f2s, f2r, cs, cr, s3, r3, xs, xr,
):
    net = Net()
    sec, zh, c, me = net.sec, net.zh, net.core, net.me

    loads = [
        pltpu.make_async_copy(src, dst, w_sem.at[i])
        for i, (src, dst) in enumerate(((w_out, wo), (w_gate, wg), (w_up, wu), (w_down, wd)))
    ]
    for load in loads:
        load.start()

    barrier = pltpu.get_barrier_semaphore()
    for axis in LAYOUT:
        for k in (1, 2, 3):
            pl.semaphore_signal(barrier, 1, device_id=net.shifted(axis, k), device_id_type=MESH)
    pl.semaphore_signal(barrier, 1, device_id=net.sibling, device_id_type=MESH)
    pl.semaphore_wait(barrier, 10)

    A[zh, c, me["y"], me["x"]] = attn[...]
    every = (1, 2, 3)
    rows_gather = Gather(
        net, A, {"z": zh, "y": me["y"], "x": me["x"]}, {"z": (2,), "y": every, "x": every},
        PARTS, (0, 256), (s1, r1, f1s, f1r), 0,
    )
    rows_gather.start()

    loads[1].wait()
    loads[2].wait()

    def scale(i, _):
        cols = pl.ds(pl.multiple_of(i * 256, 256), 256)
        g = gain[:, cols]
        wg[:, cols] = (wg[:, cols].astype(F32) * g).astype(BF16)
        wu[:, cols] = (wu[:, cols].astype(F32) * g).astype(BF16)
        return 0

    lax.fori_loop(0, D // 256, scale, 0)

    for stage in range(3):
        rows_gather.step(stage)

    loads[0].wait()

    def project(core):
        total = jnp.zeros((512, 256), F32)
        for j in range(0, 16, 2):
            lhs = jnp.concatenate(
                [A[:, core, :, :, (j + t) * 16 : (j + t + 1) * 16, :].reshape(512, 128) for t in range(2)], axis=1
            )
            rhs = jnp.concatenate(
                [
                    jnp.concatenate(
                        [wo[(2 * (j + t) + u) * 128 : (2 * (j + t) + u + 1) * 128, :] for u in range(2)], axis=1
                    )
                    for t in range(2)
                ],
                axis=0,
            )
            total = total + jnp.dot(lhs, rhs, preferred_element_type=F32)
        total = total.reshape(32, 2, 8, 256)
        mixed[:, core] = (total[:, 0, :, :128] + total[:, 1, :, 128:]).reshape(2, 128, 128)

    project(c)
    rows_gather.finish()
    project(1 - c)

    sec_out[...] = mixed[1 - sec].reshape(256, 128).astype(BF16)
    swap = net.copy(sec_out, sec_in, xs.at[0], xr.at[0], net.partner)
    swap.start()
    half_rows = pl.ds(pl.multiple_of(sec * 256, 256), 256)
    own = residual[half_rows, :].astype(F32)
    swap.wait_recv()
    X[me["z"], c, me["y"], me["x"]] = (
        own + (mixed[sec].reshape(256, 128) + sec_in[...].astype(F32))
    ).astype(BF16)

    gathers = [
        Gather(
            net, X, me, {"z": every, "y": every, "x": every}, HALF_PARTS[h], (h * HALF, HALF), (s2, r2, f2s, f2r), h
        )
        for h in range(2)
    ]
    scatters = [Scatter(net, Q, (R1, R2, R3), HALF_PARTS[h], (s3, r3), h) for h in range(2)]

    def ffn_in(h, core, first):
        rows = pl.ds(h * HALF, HALF)
        if first:
            acc_g[...] = jnp.zeros_like(acc_g)
            acc_u[...] = jnp.zeros_like(acc_u)
            acc_s[...] = jnp.zeros_like(acc_s)

        def body(hi, _):
            cols = pl.ds(pl.multiple_of((hi * 2 + core) * 2048, 2048), 2048)
            halves = []
            for lo in range(2):
                blocks = [X[hi * 2 + lo, core, b // 4, b % 4, rows] for b in range(16)]
                squares = acc_s[lo * HALF : (lo + 1) * HALF]
                for b in blocks:
                    wide = b.astype(F32)
                    squares = squares + wide * wide
                acc_s[lo * HALF : (lo + 1) * HALF] = squares
                halves.append(jnp.concatenate(blocks, axis=1))
            lhs = jnp.concatenate(halves, axis=0)
            nt = (((1,), (1,)), ((), ()))
            acc_g[...] += lax.dot_general(lhs, wg[:, cols], nt, preferred_element_type=F32)
            acc_u[...] += lax.dot_general(lhs, wu[:, cols], nt, preferred_element_type=F32)
            return 0

        lax.fori_loop(0, 2, body, 0)

    def activate():
        inv = lax.rsqrt(jnp.sum(acc_s[...], axis=1, keepdims=True) / D + EPS)
        gate = acc_g[...] * inv
        hidden[...] = (gate / (1.0 + jnp.exp(-gate)) * (acc_u[...] * inv)).astype(BF16)

    def core_copy(h, i):
        hi, y = i // 4, i % 4
        rows = pl.ds(h * HALF, HALF)
        return net.copy(
            Q.at[pl.ds(hi * 2, 2), 1 - c, y, :, rows], RC.at[pl.ds(hi * 2, 2), y, :, rows],
            cs.at[h * 8 + i], cr.at[h * 8 + i], net.sibling,
        )

    def ffn_out(h):
        rows = pl.ds(h * HALF, HALF)

        def tile(core, hi):
            cols = pl.ds(pl.multiple_of((hi * 2 + core) * 2048, 2048), 2048)
            part = jnp.dot(hidden[...], wd[:, cols], preferred_element_type=F32)
            for lo in range(2):
                for y in range(4):
                    for x in range(4):
                        Q[hi * 2 + lo, core, y, x, rows] = part[
                            lo * HALF : (lo + 1) * HALF, (y * 4 + x) * 128 : (y * 4 + x + 1) * 128
                        ].astype(BF16)

        for hi in range(2):
            tile(1 - c, hi)
            for y in range(4):
                core_copy(h, hi * 4 + y).start()
        for hi in range(2):
            tile(c, hi)

        def add_sibling(i, _):
            hi, y = i // 4, i % 4
            core_copy(h, i).wait_recv()
            for lo in range(2):
                z = hi * 2 + lo
                for x in range(4):
                    Q[z, c, y, x, rows] = (Q[z, c, y, x, rows].astype(F32) + RC[z, y, x, rows].astype(F32)).astype(
                        BF16
                    )
            return 0

        lax.fori_loop(0, 8, add_sibling, 0)

    def close(h):
        rows = pl.ds(h * HALF, HALF)
        total = X[me["z"], c, me["y"], me["x"], rows].astype(F32)
        ffn = Q[me["z"], c, me["y"], me["x"], rows].astype(F32)
        for k in range(3):
            ffn = ffn + R3[k, rows].astype(F32)
        done = (total + ffn).astype(BF16)
        fin_out[rows] = done
        last = net.copy(fin_out.at[rows], fin_in.at[rows], xs.at[1 + h], xr.at[1 + h], net.partner)
        last.start()
        out_ref[pl.ds(pl.multiple_of(sec * 256 + h * HALF, HALF), HALF), :] = done
        return last

    g0, g1 = gathers
    t0, t1 = scatters
    g0.start()
    g0.step(0)
    g1.start()
    g0.step(1)
    g1.step(0)
    g1.step(1)
    g0.step(2)
    ffn_in(0, c, True)
    g0.finish()
    ffn_in(0, 1 - c, False)
    activate()
    loads[3].wait()
    ffn_out(0)
    t0.start()
    g1.step(2)
    ffn_in(1, c, True)
    g1.finish()
    ffn_in(1, 1 - c, False)
    activate()
    ffn_out(1)
    t1.start()
    t0.step(0)
    t0.step(1)
    t1.step(0)
    t0.step(2)
    last0 = close(0)
    t1.step(1)
    t1.step(2)
    last1 = close(1)

    swap.wait_send()
    for part in (rows_gather, g0, g1, t0, t1):
        part.drain()
    for h in range(2):

        def sent(i, _, h=h):
            core_copy(h, i).wait_send()
            return 0

        lax.fori_loop(0, 8, sent, 0)
    last0.wait()
    last1.wait()
    out_ref[pl.ds(pl.multiple_of((1 - sec) * 256, 256), 256), :] = fin_in[...]


def rest(attn, residual, gain, w_out, w_gate, w_up, w_down):
    vmem = pl.BlockSpec(memory_space=pltpu.VMEM)
    anywhere = pl.BlockSpec(memory_space=pl.ANY)
    dma = pltpu.SemaphoreType.DMA
    return pl.pallas_call(
        layer,
        out_shape=jax.ShapeDtypeStruct((512, 128), BF16),
        in_specs=[vmem, vmem, vmem, anywhere, anywhere, anywhere, anywhere],
        out_specs=vmem,
        scratch_shapes=[
            pltpu.VMEM((2, 2, 4, 4, 256, 128), BF16),
            pltpu.VMEM((4, 2, 4, 4, 256, 128), BF16),
            pltpu.VMEM((4, 2, 4, 4, 256, 128), BF16),
            pltpu.VMEM((4, 4, 4, 256, 128), BF16),
            pltpu.VMEM((3, 4, 4, 256, 128), BF16),
            pltpu.VMEM((3, 4, 256, 128), BF16),
            pltpu.VMEM((3, 256, 128), BF16),
            pltpu.VMEM((256, 128), BF16),
            pltpu.VMEM((256, 128), BF16),
            pltpu.VMEM((256, 128), BF16),
            pltpu.VMEM((256, 128), BF16),
            pltpu.VMEM(w_out.shape, BF16),
            pltpu.VMEM(w_gate.shape, BF16),
            pltpu.VMEM(w_up.shape, BF16),
            pltpu.VMEM(w_down.shape, BF16),
            pltpu.VMEM((256, w_gate.shape[0]), F32),
            pltpu.VMEM((256, w_gate.shape[0]), F32),
            pltpu.VMEM((256, 128), F32),
            pltpu.VMEM((256, w_gate.shape[0]), BF16),
            pltpu.VMEM((2, 2, 128, 128), F32),
            dma((4,)),
            dma((27,)), dma((27,)), dma((28,)), dma((28,)),
            dma((54,)), dma((54,)), dma((56,)), dma((56,)),
            dma((16,)), dma((16,)),
            dma((54,)), dma((54,)),
            dma((3,)), dma((3,)),
        ],
        compiler_params=pltpu.CompilerParams(collective_id=0, has_side_effects=True, vmem_limit_bytes=60 << 20),
        name="layer_rest",
    )(attn, residual, gain, w_out, w_gate, w_up, w_down)


def per_device(
    queries, new_token_pairs, paged_cache_store, page_table, cache_lengths,
    out_weight, residual, norm_gain, gate_weight, up_weight, down_weight,
):
    attn = attention(queries, new_token_pairs, paged_cache_store, page_table, cache_lengths)
    return rest(attn, residual, norm_gain.reshape(1, D), out_weight, gate_weight, up_weight, down_weight)


def solution(mesh):
    in_specs = (
        P(("grp", "tp"), None, "sec"),
        P(("grp", "tp"), None, None, "sec"),
        P(("grp", "tp"), None, None, "sec"),
        P(("grp", "tp"), None),
        P(("grp", "tp")),
        P("sec", ("grp", "tp")),
        P(None, ("grp", "tp")),
        P(),
        P(("sec", "grp", "tp"), None),
        P(("sec", "grp", "tp"), None),
        P(("sec", "grp", "tp"), None),
    )
    out_specs = P(None, ("grp", "tp"))
    return jax.shard_map(
        per_device, mesh=mesh, in_specs=in_specs, out_specs=out_specs, check_vma=False
    )
```

```python
import functools
import math

import jax
import jax.numpy as jnp
from jax import lax
from jax.experimental import pallas as pl
from jax.experimental.pallas import tpu as pltpu
from jax.sharding import PartitionSpec as P

D = 8192
HEAD_SIZE = 128
EPS = 1e-05
MESH = pl.DeviceIdType.MESH
F32 = jnp.float32
BF16 = jnp.bfloat16

PAGE = 64
CHUNK_PAGES = 8
CHUNK = PAGE * CHUNK_PAGES
MAXLEN = 3072
REQS = 2
KV_HEADS = 4
GROUP = 8
TOKENS = 4
NEW_ROWS = REQS * TOKENS * 2

PARTS = ((0, 64), (64, 96), (160, 96))
HALF_PARTS = (((0, 48), (48, 48), (96, 32)), ((128, 32), (160, 48), (208, 48)))
HALF = 128
ORDERS = (("x", "y", "z"), ("y", "z", "x"), ("z", "x", "y"))
LAYOUT = ("z", "y", "x")


def attend(table, lengths, q_ref, new_ref, kv_ref, out_ref, flat, new_flat, s_buf, acc, o32, sems, new_sems):
    kv_rows = kv_ref.reshape(kv_ref.shape[0], 2 * PAGE, KV_HEADS * HEAD_SIZE)
    new_rows = new_ref.reshape(NEW_ROWS, KV_HEADS * HEAD_SIZE)
    factor = 1.0 / math.sqrt(HEAD_SIZE)
    rows = GROUP * TOKENS
    queries = KV_HEADS * rows
    nt = (((1,), (1,)), ((), ()))

    new_copies = []
    new_flat[:, pl.ds(NEW_ROWS, 128 - NEW_ROWS), :] = jnp.zeros((KV_HEADS, 128 - NEW_ROWS, HEAD_SIZE), BF16)
    for h in range(KV_HEADS):
        copy = pltpu.make_async_copy(
            new_rows.at[:, pl.ds(h * HEAD_SIZE, HEAD_SIZE)], new_flat.at[h, pl.ds(0, NEW_ROWS)], new_sems.at[h]
        )
        copy.start()
        new_copies.append(copy)

    for r in range(REQS):
        chunks = (lengths[r] + CHUNK - 1) // CHUNK

        def start(p, _, r=r):
            page = table[r, p]
            for h in range(KV_HEADS):
                pltpu.make_async_copy(
                    kv_rows.at[page, :, pl.ds(h * HEAD_SIZE, HEAD_SIZE)],
                    flat.at[h, r, pl.ds(pl.multiple_of(p * 2 * PAGE, 2 * PAGE), 2 * PAGE)],
                    sems.at[r, p // CHUNK_PAGES],
                ).start()
            return 0

        lax.fori_loop(0, chunks * CHUNK_PAGES, start, 0)

    stacked = []
    for r in range(REQS):
        wide = q_ref[r].astype(F32)
        blocks = []
        for h in range(KV_HEADS):
            q = jnp.concatenate(
                [wide[:, (h * GROUP + g) * HEAD_SIZE : (h * GROUP + g + 1) * HEAD_SIZE] for g in range(GROUP)], axis=0
            ).astype(BF16)
            zero = jnp.zeros_like(q)
            blocks.append(jnp.concatenate([q if k == h else zero for k in range(KV_HEADS)], axis=1))
        stacked.append(jnp.concatenate(blocks, axis=0))

    def pairs(r, first, count):
        return jnp.concatenate([flat[h, r, pl.ds(first, count), :] for h in range(KV_HEADS)], axis=1)

    col = lax.broadcasted_iota(jnp.int32, (queries, 128), 1)
    row = lax.broadcasted_iota(jnp.int32, (queries, 128), 0)
    wide_col = lax.broadcasted_iota(jnp.int32, (8, 2 * CHUNK), 1)
    place = jnp.where(wide_col % 2 == 0, wide_col, 2 * MAXLEN)[:1]

    for copy in new_copies:
        copy.wait()
    new_pairs = jnp.concatenate([new_flat[h] for h in range(KV_HEADS)], axis=1)
    fresh = []
    for r in range(REQS):
        s = lax.dot_general(stacked[r], new_pairs, nt, preferred_element_type=F32)
        token = (col - r * 2 * TOKENS) // 2
        live = (col % 2 == 0) & (col >= r * 2 * TOKENS) & (token <= row % TOKENS)
        fresh.append(jnp.where(live, s * factor, -jnp.inf))

    for r in range(REQS):
        length = lengths[r]
        chunks = (length + CHUNK - 1) // CHUNK
        q = stacked[r]

        def score(c, peak, r=r, q=q, length=length):
            here = flat.at[:, r, pl.ds(pl.multiple_of(c * 2 * CHUNK, 2 * CHUNK), 2 * CHUNK)]
            pltpu.make_async_copy(
                here, here, sems.at[r, c]
            ).wait()
            s = lax.dot_general(
                q, pairs(r, pl.multiple_of(c * 2 * CHUNK, 2 * CHUNK), 2 * CHUNK), nt, preferred_element_type=F32
            )
            s = jnp.where(place < 2 * (length - c * CHUNK), s * factor, -jnp.inf)
            s_buf[c] = s
            for t in range(2 * CHUNK // 128):
                peak = jnp.maximum(peak, s[:, t * 128 : (t + 1) * 128])
            return peak

        peak = jnp.max(lax.fori_loop(0, chunks, score, fresh[r]), axis=1, keepdims=True)

        w = jnp.exp(fresh[r] - peak)
        acc[...] = jnp.dot(
            pltpu.roll(w, 1, 1).astype(BF16), new_pairs, preferred_element_type=F32
        )

        def weigh(c, total, r=r, peak=peak):
            moved = []
            for t in range(2 * CHUNK // 128):
                w = jnp.exp(s_buf[c, :, t * 128 : (t + 1) * 128] - peak)
                total = total + w
                moved.append(pltpu.roll(w, 1, 1).astype(BF16))
            acc[...] += jnp.dot(
                jnp.concatenate(moved, axis=1),
                pairs(r, pl.multiple_of(c * 2 * CHUNK, 2 * CHUNK), 2 * CHUNK),
                preferred_element_type=F32,
            )
            return total

        total = jnp.sum(lax.fori_loop(0, chunks, weigh, w), axis=1, keepdims=True)
        for h in range(KV_HEADS):
            here = slice(h * rows, (h + 1) * rows)
            out = acc[here, h * HEAD_SIZE : (h + 1) * HEAD_SIZE] / total[here]
            for g in range(GROUP):
                o32[h * GROUP + g, r * TOKENS : (r + 1) * TOKENS, :] = out[g * TOKENS : (g + 1) * TOKENS]
    out_ref[...] = o32[...].reshape(KV_HEADS * GROUP * REQS * TOKENS, HEAD_SIZE).astype(BF16)


def attention(queries, new_token_pairs, paged_cache_store, page_table, cache_lengths):
    smem = pl.BlockSpec(memory_space=pltpu.SMEM)
    vmem = pl.BlockSpec(memory_space=pltpu.VMEM)
    anywhere = pl.BlockSpec(memory_space=pl.ANY)
    return pl.pallas_call(
        attend,
        out_shape=jax.ShapeDtypeStruct((256, HEAD_SIZE), BF16),
        in_specs=[smem, smem, vmem, anywhere, anywhere],
        out_specs=vmem,
        scratch_shapes=[
            pltpu.VMEM((KV_HEADS, REQS, 2 * MAXLEN, HEAD_SIZE), BF16),
            pltpu.VMEM((KV_HEADS, 128, HEAD_SIZE), BF16),
            pltpu.VMEM((MAXLEN // CHUNK, KV_HEADS * GROUP * TOKENS, 2 * CHUNK), F32),
            pltpu.VMEM((KV_HEADS * GROUP * TOKENS, KV_HEADS * HEAD_SIZE), F32),
            pltpu.VMEM((KV_HEADS * GROUP, REQS * TOKENS, HEAD_SIZE), F32),
            pltpu.SemaphoreType.DMA((REQS, MAXLEN // CHUNK)),
            pltpu.SemaphoreType.DMA((KV_HEADS,)),
        ],
        compiler_params=pltpu.CompilerParams(vmem_limit_bytes=58 << 20),
        name="paged_attention",
    )(page_table, cache_lengths, queries, new_token_pairs, paged_cache_store)


def split(at, size):
    first = next(a for a in LAYOUT if isinstance(at[a], slice))
    half = size[first] // 2
    return first, ({**at, first: pl.ds(0, half)}, {**at, first: pl.ds(half, half)})


class Gather:
    def __init__(self, net, buf, coord, offsets, parts, sems, base):
        self.net, self.buf, self.coord, self.offsets, self.parts = net, buf, coord, offsets, parts
        self.size = {"z": buf.shape[0], "y": buf.shape[2], "x": buf.shape[3]}
        self.send, self.recv, self.fsend, self.frecv = sems
        self.base, self.fbase = base * 36, base * 36
        self.held = [dict(coord) for _ in parts]
        self.pending = [[] for _ in parts]
        self.flying, self.forwards = [], []

    def region(self, at, rows):
        return self.buf.at[at["z"], self.net.core, at["y"], at["x"], pl.ds(*rows)]

    def forward(self, at, rows, slot):
        part = self.region(at, rows)
        slot = self.fbase + slot
        copy = self.net.copy(part, part, self.fsend.at[slot], self.frecv.at[slot], self.net.sibling)
        copy.start()
        self.forwards.append(copy)

    def push(self, p, slot, at, axis, k):
        slot = p * 12 + slot
        block = self.region(at, self.parts[p])
        copy = self.net.copy(
            block, block, self.send.at[self.base + slot], self.recv.at[self.base + slot], self.net.shifted(axis, k)
        )
        copy.start()
        self.flying.append(copy)
        return copy, slot

    def came(self, axis, k):
        return (self.coord[axis] + 4 - k) % 4 if self.size[axis] == 4 else 1 - self.coord[axis]

    def ring(self, p):
        return len(self.offsets[ORDERS[p][2]]) == 3

    def launch(self, p, stage):
        axis = ORDERS[p][stage]
        held = self.held[p]
        if stage == 2 and self.ring(p):
            _, (low, high) = split(held, self.size)
            for slot, at, k in ((6, low, 1), (7, high, 3), (8, high, 1), (9, low, 3)):
                copy, slot = self.push(p, slot, at, axis, k)
                self.pending[p].append((copy, slot, {**at, axis: self.came(axis, k)}, k))
            return
        for k in self.offsets[axis]:
            copy, slot = self.push(p, stage * 3 + k - 1, held, axis, k)
            self.pending[p].append((copy, slot, {**held, axis: self.came(axis, k)}, k))

    def start(self):
        for p in range(3):
            self.launch(p, 0)

    def land(self, p, count):
        arrived, self.pending[p] = self.pending[p][:count], self.pending[p][count:]
        for copy, *_ in arrived:
            copy.wait_recv()
        return arrived

    def step(self, stage):
        for p in range(3):
            arrived = self.land(p, len(self.pending[p]))
            if stage < 2:
                axis = ORDERS[p][stage]
                self.held[p] = {**self.held[p], axis: slice(None)}
                self.launch(p, stage + 1)
            else:
                for _, slot, at, _ in arrived:
                    self.forward(at, self.parts[p], slot)
        if stage == 1:
            for p in range(3):
                self.forward(self.held[p], self.parts[p], p * 12)

    def relay(self):
        landed = []
        for p in range(3):
            if not self.ring(p):
                continue
            axis = ORDERS[p][2]
            arrived = self.land(p, 2)
            for (_, _, at, k), slot in zip(arrived, (10, 11)):
                copy, slot = self.push(p, slot, at, axis, k)
                self.pending[p].append((copy, slot, {**at, axis: self.came(axis, 2)}, k))
            landed.append((p, arrived))
        for p, arrived in landed:
            for _, slot, at, _ in arrived:
                self.forward(at, self.parts[p], slot)

    def finish(self):
        for copy in self.forwards:
            copy.wait_recv()

    def drain(self):
        for copy in self.flying + self.forwards:
            copy.wait_send()


class Scatter:
    def __init__(self, net, Q, landing, parts, sems, base):
        self.net, self.Q, self.landing, self.parts = net, Q, landing, parts
        self.send, self.recv = sems
        self.base = base * 36
        self.pending = [[] for _ in parts]
        self.flying = []

    def push(self, p, slot, src, dst, axis, k):
        slot = self.base + p * 12 + slot
        copy = self.net.copy(src, dst, self.send.at[slot], self.recv.at[slot], self.net.shifted(axis, k))
        copy.start()
        self.flying.append(copy)
        self.pending[p].append(copy)

    def part(self, p, at):
        return self.Q.at[at["z"], self.net.core, at["y"], at["x"], pl.ds(*self.parts[p])]

    def first(self, p):
        order = ORDERS[p][::-1]
        axis = order[0]
        whole = {a: (self.net.me[a] if a == axis else slice(None)) for a in LAYOUT}
        return axis, split(whole, {a: 4 for a in LAYOUT})[1], [a for a in LAYOUT if a != axis]

    def start(self):
        for p in range(3):
            axis, halves, left = self.first(p)
            rows = pl.ds(*self.parts[p])
            me = self.net.me[axis]
            for slot, half, away, k, land in ((0, 0, 2, 1, 2), (1, 1, 2, 3, 2), (2, 1, 1, 1, 0), (3, 0, 3, 3, 1)):
                at = {**halves[half], axis: (me + away) % 4}
                dst = self.landing[0].at[land, pl.ds(half * 2, 2), :, rows]
                self.push(p, slot, self.part(p, at), dst, axis, k)

    def relay(self):
        for p in range(3):
            axis, halves, left = self.first(p)
            rows = pl.ds(*self.parts[p])
            me = self.net.me[axis]
            arrived, self.pending[p] = self.pending[p][:2], self.pending[p][2:]
            for slot, half, k, land in ((4, 0, 1, 0), (5, 1, 3, 1)):
                arrived[half].wait_recv()
                target = (me + k) % 4

                def add(i, _, half=half, rows=rows, target=target, axis=axis, left=left):
                    where = (half * 2 + i // 4, i % 4)
                    at = {axis: target, **dict(zip(left, where))}
                    got = self.landing[0][2, where[0], where[1], rows].astype(F32)
                    spot = (at["z"], self.net.core, at["y"], at["x"], rows)
                    self.Q[spot] = (self.Q[spot].astype(F32) + got).astype(BF16)
                    return 0

                lax.fori_loop(0, 8, add, 0)
                dst = self.landing[0].at[land, pl.ds(half * 2, 2), :, rows]
                self.push(p, slot, self.part(p, {**halves[half], axis: target}), dst, axis, k)

    def launch(self, p, stage):
        order = ORDERS[p][::-1]
        axis, left = order[stage], order[stage + 1 :]
        me = self.net.me
        for k in (1, 2, 3):
            at = {a: (slice(None) if a in left else me[a]) for a in LAYOUT}
            at[axis] = (me[axis] + k) % 4
            dst = self.landing[stage].at[(k - 1, *(slice(None),) * len(left), pl.ds(*self.parts[p]))]
            self.push(p, 3 + stage * 3 + k - 1, self.part(p, at), dst, axis, k)

    def step(self, stage):
        for p in range(3):
            order = ORDERS[p][::-1]
            left = [a for a in LAYOUT if a in order[stage + 1 :]]
            rows = pl.ds(*self.parts[p])
            me, core, Q = self.net.me, self.net.core, self.Q
            land = self.landing[stage]
            for copy in self.pending[p]:
                copy.wait_recv()
            self.pending[p] = []
            if stage == 2:
                continue

            def add(i, _, left=left, rows=rows, land=land):
                where = (i // 4, i % 4) if stage == 0 else (i,)
                at = {**me, **dict(zip(left, where))}
                total = Q[at["z"], core, at["y"], at["x"], rows].astype(F32)
                for k in range(2 if stage == 0 else 3):
                    got = land[k, where[0], where[1], rows] if stage == 0 else land[k, where[0], rows]
                    total = total + got.astype(F32)
                Q[at["z"], core, at["y"], at["x"], rows] = total.astype(BF16)
                return 0

            lax.fori_loop(0, 16 if stage == 0 else 4, add, 0)
            self.launch(p, stage + 1)

    def drain(self):
        for copy in self.flying:
            copy.wait_send()


class Net:
    def __init__(self):
        sec, grp, tp = lax.axis_index("sec"), lax.axis_index("grp"), lax.axis_index("tp")
        self.sec, self.zh, self.core = sec, grp // 2, grp % 2
        self.me = {"z": self.zh * 2 + sec, "y": tp // 4, "x": tp % 4}
        self.sibling = self.device(self.me, 1 - self.core)
        self.partner = self.device({**self.me, "z": self.zh * 2 + (1 - sec)}, self.core)

    def device(self, at, core):
        return (at["z"] % 2, (at["z"] // 2) * 2 + core, at["y"] * 4 + at["x"])

    def shifted(self, axis, k):
        return self.device({**self.me, axis: (self.me[axis] + k) % 4}, self.core)

    def copy(self, src, dst, send, recv, to):
        return pltpu.make_async_remote_copy(src, dst, send, recv, device_id=to, device_id_type=MESH)


def layer(
    attn, residual, gain, w_out, w_gate, w_up, w_down, out_ref,
    A, X, Q, RC, R1, R2, R3, sec_in, sec_out, fin_in, fin_out,
    wo, wg, wu, wd, res, scales, acc_g, acc_u, acc_s, hidden, mixed,
    w_sem, s1, r1, f1s, f1r, s2, r2, f2s, f2r, cs, cr, s3, r3, xs, xr,
):
    net = Net()
    sec, zh, c, me = net.sec, net.zh, net.core, net.me

    barrier = pltpu.get_barrier_semaphore()
    for axis in LAYOUT:
        for k in (1, 2, 3):
            pl.semaphore_signal(barrier, 1, device_id=net.shifted(axis, k), device_id_type=MESH)
    pl.semaphore_signal(barrier, 1, device_id=net.sibling, device_id_type=MESH)

    half_rows = pl.ds(pl.multiple_of(sec * 256, 256), 256)
    loads = [
        pltpu.make_async_copy(src, dst, w_sem.at[i])
        for i, (src, dst) in enumerate(
            (
                (w_out, wo), (w_gate, wg), (w_up, wu), (w_down, wd),
                (attn, A.at[zh, c, me["y"], me["x"]]), (residual.at[half_rows], res), (gain, scales),
            )
        )
    ]
    for i in (4, 5, 6, 0, 1, 2, 3):
        loads[i].start()
    pl.semaphore_wait(barrier, 10)

    loads[4].wait()
    every = (1, 2, 3)
    rows_gather = Gather(
        net, A, {"z": zh, "y": me["y"], "x": me["x"]}, {"z": (2,), "y": every, "x": every},
        PARTS, (s1, r1, f1s, f1r), 0,
    )
    rows_gather.start()

    def scale_weights():
        for i in (1, 2, 6):
            loads[i].wait()

        def scale(i, _):
            cols = pl.ds(pl.multiple_of(i * 512, 512), 512)
            g = scales[:, cols]
            wg[:, cols] = (wg[:, cols].astype(F32) * g).astype(BF16)
            wu[:, cols] = (wu[:, cols].astype(F32) * g).astype(BF16)
            return 0

        lax.fori_loop(0, D // 512, scale, 0)

    rows_gather.step(0)
    rows_gather.step(1)
    rows_gather.relay()
    rows_gather.step(2)

    loads[0].wait()

    def project(core):
        total = jnp.zeros((512, 256), F32)
        for j in range(0, 16, 2):
            lhs = jnp.concatenate(
                [A[:, core, :, :, (j + t) * 16 : (j + t + 1) * 16, :].reshape(512, 128) for t in range(2)], axis=1
            )
            rhs = jnp.concatenate(
                [
                    jnp.concatenate(
                        [wo[(2 * (j + t) + u) * 128 : (2 * (j + t) + u + 1) * 128, :] for u in range(2)], axis=1
                    )
                    for t in range(2)
                ],
                axis=0,
            )
            total = total + jnp.dot(lhs, rhs, preferred_element_type=F32)
        total = total.reshape(32, 2, 8, 256)
        mixed[:, core] = (total[:, 0, :, :128] + total[:, 1, :, 128:]).reshape(2, 128, 128)

    project(c)
    rows_gather.finish()
    project(1 - c)

    sec_out[...] = mixed[1 - sec].reshape(256, 128).astype(BF16)
    swap = net.copy(sec_out, sec_in, xs.at[0], xr.at[0], net.partner)
    swap.start()
    loads[5].wait()
    own = res[...].astype(F32)
    swap.wait_recv()
    X[me["z"], c, me["y"], me["x"]] = (
        own + (mixed[sec].reshape(256, 128) + sec_in[...].astype(F32))
    ).astype(BF16)

    gathers = [
        Gather(
            net, X, me, {"z": every, "y": every, "x": every}, HALF_PARTS[h], (s2, r2, f2s, f2r), h
        )
        for h in range(2)
    ]
    scatters = [Scatter(net, Q, (R1, R2, R3), HALF_PARTS[h], (s3, r3), h) for h in range(2)]

    def ffn_in(h, core, first):
        rows = pl.ds(h * HALF, HALF)
        if first:
            acc_g[...] = jnp.zeros_like(acc_g)
            acc_u[...] = jnp.zeros_like(acc_u)
            acc_s[...] = jnp.zeros_like(acc_s)

        def body(hi, _):
            cols = pl.ds(pl.multiple_of((hi * 2 + core) * 2048, 2048), 2048)
            halves = []
            for lo in range(2):
                blocks = [X[hi * 2 + lo, core, b // 4, b % 4, rows] for b in range(16)]
                squares = acc_s[lo * HALF : (lo + 1) * HALF]
                for b in blocks:
                    wide = b.astype(F32)
                    squares = squares + wide * wide
                acc_s[lo * HALF : (lo + 1) * HALF] = squares
                halves.append(jnp.concatenate(blocks, axis=1))
            lhs = jnp.concatenate(halves, axis=0)
            nt = (((1,), (1,)), ((), ()))
            acc_g[...] += lax.dot_general(lhs, wg[:, cols], nt, preferred_element_type=F32)
            acc_u[...] += lax.dot_general(lhs, wu[:, cols], nt, preferred_element_type=F32)
            return 0

        lax.fori_loop(0, 2, body, 0)

    def activate():
        inv = lax.rsqrt(jnp.sum(acc_s[...], axis=1, keepdims=True) / D + EPS)
        gate = acc_g[...] * inv
        hidden[...] = (gate / (1.0 + jnp.exp(-gate)) * (acc_u[...] * inv)).astype(BF16)

    def core_copy(h, i):
        hi, y = i // 4, i % 4
        rows = pl.ds(h * HALF, HALF)
        return net.copy(
            Q.at[pl.ds(hi * 2, 2), 1 - c, y, :, rows], RC.at[pl.ds(hi * 2, 2), y, :, rows],
            cs.at[h * 8 + i], cr.at[h * 8 + i], net.sibling,
        )

    def ffn_out(h):
        rows = pl.ds(h * HALF, HALF)

        def tile(core, hi):
            cols = pl.ds(pl.multiple_of((hi * 2 + core) * 2048, 2048), 2048)
            part = jnp.dot(hidden[...], wd[:, cols], preferred_element_type=F32)
            for lo in range(2):
                for y in range(4):
                    for x in range(4):
                        Q[hi * 2 + lo, core, y, x, rows] = part[
                            lo * HALF : (lo + 1) * HALF, (y * 4 + x) * 128 : (y * 4 + x + 1) * 128
                        ].astype(BF16)

        for hi in range(2):
            tile(1 - c, hi)
            for y in range(4):
                core_copy(h, hi * 4 + y).start()
        for hi in range(2):
            tile(c, hi)

        def add_sibling(i, _):
            hi, y = i // 4, i % 4
            core_copy(h, i).wait_recv()
            for lo in range(2):
                z = hi * 2 + lo
                for x in range(4):
                    Q[z, c, y, x, rows] = (Q[z, c, y, x, rows].astype(F32) + RC[z, y, x, rows].astype(F32)).astype(
                        BF16
                    )
            return 0

        lax.fori_loop(0, 8, add_sibling, 0)

    def close(h):
        rows = pl.ds(h * HALF, HALF)
        total = X[me["z"], c, me["y"], me["x"], rows].astype(F32)
        ffn = Q[me["z"], c, me["y"], me["x"], rows].astype(F32)
        for k in range(3):
            ffn = ffn + R3[k, rows].astype(F32)
        done = (total + ffn).astype(BF16)
        fin_out[rows] = done
        last = net.copy(fin_out.at[rows], fin_in.at[rows], xs.at[1 + h], xr.at[1 + h], net.partner)
        last.start()
        out_ref[pl.ds(pl.multiple_of(sec * 256 + h * HALF, HALF), HALF), :] = done
        return last

    g0, g1 = gathers
    t0, t1 = scatters
    g0.start()
    g0.step(0)
    g1.start()
    g0.step(1)
    g1.step(0)
    g0.relay()
    g1.step(1)
    scale_weights()
    g0.step(2)
    ffn_in(0, c, True)
    g0.finish()
    ffn_in(0, 1 - c, False)
    g1.relay()
    activate()
    loads[3].wait()
    ffn_out(0)
    t0.start()
    g1.step(2)
    ffn_in(1, c, True)
    g1.finish()
    t0.relay()
    ffn_in(1, 1 - c, False)
    activate()
    ffn_out(1)
    t1.start()
    t0.step(0)
    t1.relay()
    t0.step(1)
    t1.step(0)
    t0.step(2)
    last0 = close(0)
    t1.step(1)
    t1.step(2)
    last1 = close(1)

    swap.wait_send()
    for part in (rows_gather, g0, g1, t0, t1):
        part.drain()
    for h in range(2):

        def sent(i, _, h=h):
            core_copy(h, i).wait_send()
            return 0

        lax.fori_loop(0, 8, sent, 0)
    last0.wait()
    last1.wait()
    out_ref[pl.ds(pl.multiple_of((1 - sec) * 256, 256), 256), :] = fin_in[...]


def rest(attn, residual, gain, w_out, w_gate, w_up, w_down):
    vmem = pl.BlockSpec(memory_space=pltpu.VMEM)
    anywhere = pl.BlockSpec(memory_space=pl.ANY)
    dma = pltpu.SemaphoreType.DMA
    return pl.pallas_call(
        layer,
        out_shape=jax.ShapeDtypeStruct((512, 128), BF16),
        in_specs=[anywhere] * 7,
        out_specs=vmem,
        scratch_shapes=[
            pltpu.VMEM((2, 2, 4, 4, 256, 128), BF16),
            pltpu.VMEM((4, 2, 4, 4, 256, 128), BF16),
            pltpu.VMEM((4, 2, 4, 4, 256, 128), BF16),
            pltpu.VMEM((4, 4, 4, 256, 128), BF16),
            pltpu.VMEM((3, 4, 4, 256, 128), BF16),
            pltpu.VMEM((3, 4, 256, 128), BF16),
            pltpu.VMEM((3, 256, 128), BF16),
            pltpu.VMEM((256, 128), BF16),
            pltpu.VMEM((256, 128), BF16),
            pltpu.VMEM((256, 128), BF16),
            pltpu.VMEM((256, 128), BF16),
            pltpu.VMEM(w_out.shape, BF16),
            pltpu.VMEM(w_gate.shape, BF16),
            pltpu.VMEM(w_up.shape, BF16),
            pltpu.VMEM(w_down.shape, BF16),
            pltpu.VMEM((256, 128), BF16),
            pltpu.VMEM((1, D), F32),
            pltpu.VMEM((256, w_gate.shape[0]), F32),
            pltpu.VMEM((256, w_gate.shape[0]), F32),
            pltpu.VMEM((256, 128), F32),
            pltpu.VMEM((256, w_gate.shape[0]), BF16),
            pltpu.VMEM((2, 2, 128, 128), F32),
            dma((7,)),
            dma((36,)), dma((36,)), dma((36,)), dma((36,)),
            dma((72,)), dma((72,)), dma((72,)), dma((72,)),
            dma((16,)), dma((16,)),
            dma((72,)), dma((72,)),
            dma((3,)), dma((3,)),
        ],
        compiler_params=pltpu.CompilerParams(collective_id=0, has_side_effects=True, vmem_limit_bytes=60 << 20),
        name="layer_rest",
    )(attn, residual, gain, w_out, w_gate, w_up, w_down)


def per_device(
    queries, new_token_pairs, paged_cache_store, page_table, cache_lengths,
    out_weight, residual, norm_gain, gate_weight, up_weight, down_weight,
):
    attn = attention(queries, new_token_pairs, paged_cache_store, page_table, cache_lengths)
    return rest(attn, residual, norm_gain.reshape(1, D), out_weight, gate_weight, up_weight, down_weight)


def solution(mesh):
    in_specs = (
        P(("grp", "tp"), None, "sec"),
        P(("grp", "tp"), None, None, "sec"),
        P(("grp", "tp"), None, None, "sec"),
        P(("grp", "tp"), None),
        P(("grp", "tp")),
        P("sec", ("grp", "tp")),
        P(None, ("grp", "tp")),
        P(),
        P(("sec", "grp", "tp"), None),
        P(("sec", "grp", "tp"), None),
        P(("sec", "grp", "tp"), None),
    )
    out_specs = P(None, ("grp", "tp"))
    return jax.shard_map(
        per_device, mesh=mesh, in_specs=in_specs, out_specs=out_specs, check_vma=False
    )
```

```python
import functools
import math

import jax
import jax.numpy as jnp
from jax import lax
from jax.experimental import pallas as pl
from jax.experimental.pallas import tpu as pltpu
from jax.sharding import PartitionSpec as P

D = 8192
HEAD_SIZE = 128
EPS = 1e-05
MESH = pl.DeviceIdType.MESH
F32 = jnp.float32
BF16 = jnp.bfloat16

PAGE = 64
CHUNK_PAGES = 8
CHUNK = PAGE * CHUNK_PAGES
MAXLEN = 3072
REQS = 2
KV_HEADS = 4
GROUP = 8
TOKENS = 4
NEW_ROWS = REQS * TOKENS * 2

PARTS = ((0, 64), (64, 96), (160, 96))
HALF_PARTS = (((0, 48), (48, 48), (96, 32)), ((128, 32), (160, 48), (208, 48)))
HALF = 128
ORDERS = (("x", "y", "z"), ("y", "z", "x"), ("z", "x", "y"))
LAYOUT = ("z", "y", "x")


def attend(table, lengths, q_ref, new_ref, kv_ref, out_ref, flat, new_flat, s_buf, acc, o32, sems, new_sems):
    kv_rows = kv_ref.reshape(kv_ref.shape[0], 2 * PAGE, KV_HEADS * HEAD_SIZE)
    new_rows = new_ref.reshape(NEW_ROWS, KV_HEADS * HEAD_SIZE)
    factor = 1.0 / math.sqrt(HEAD_SIZE)
    rows = GROUP * TOKENS
    queries = KV_HEADS * rows
    nt = (((1,), (1,)), ((), ()))

    new_copies = []
    new_flat[:, pl.ds(NEW_ROWS, 128 - NEW_ROWS), :] = jnp.zeros((KV_HEADS, 128 - NEW_ROWS, HEAD_SIZE), BF16)
    for h in range(KV_HEADS):
        copy = pltpu.make_async_copy(
            new_rows.at[:, pl.ds(h * HEAD_SIZE, HEAD_SIZE)], new_flat.at[h, pl.ds(0, NEW_ROWS)], new_sems.at[h]
        )
        copy.start()
        new_copies.append(copy)

    for r in range(REQS):
        chunks = (lengths[r] + CHUNK - 1) // CHUNK

        def start(p, _, r=r):
            page = table[r, p]
            for h in range(KV_HEADS):
                pltpu.make_async_copy(
                    kv_rows.at[page, :, pl.ds(h * HEAD_SIZE, HEAD_SIZE)],
                    flat.at[h, r, pl.ds(pl.multiple_of(p * 2 * PAGE, 2 * PAGE), 2 * PAGE)],
                    sems.at[r, p // CHUNK_PAGES],
                ).start()
            return 0

        lax.fori_loop(0, chunks * CHUNK_PAGES, start, 0)

    stacked = []
    for r in range(REQS):
        wide = q_ref[r].astype(F32)
        blocks = []
        for h in range(KV_HEADS):
            q = jnp.concatenate(
                [wide[:, (h * GROUP + g) * HEAD_SIZE : (h * GROUP + g + 1) * HEAD_SIZE] for g in range(GROUP)], axis=0
            ).astype(BF16)
            zero = jnp.zeros_like(q)
            blocks.append(jnp.concatenate([q if k == h else zero for k in range(KV_HEADS)], axis=1))
        stacked.append(jnp.concatenate(blocks, axis=0))

    def pairs(r, first, count):
        return jnp.concatenate([flat[h, r, pl.ds(first, count), :] for h in range(KV_HEADS)], axis=1)

    col = lax.broadcasted_iota(jnp.int32, (queries, 128), 1)
    row = lax.broadcasted_iota(jnp.int32, (queries, 128), 0)
    wide_col = lax.broadcasted_iota(jnp.int32, (8, 2 * CHUNK), 1)
    place = jnp.where(wide_col % 2 == 0, wide_col, 2 * MAXLEN)[:1]

    for copy in new_copies:
        copy.wait()
    new_pairs = jnp.concatenate([new_flat[h] for h in range(KV_HEADS)], axis=1)
    fresh = []
    for r in range(REQS):
        s = lax.dot_general(stacked[r], new_pairs, nt, preferred_element_type=F32)
        token = (col - r * 2 * TOKENS) // 2
        live = (col % 2 == 0) & (col >= r * 2 * TOKENS) & (token <= row % TOKENS)
        fresh.append(jnp.where(live, s * factor, -jnp.inf))

    for r in range(REQS):
        length = lengths[r]
        chunks = (length + CHUNK - 1) // CHUNK
        q = stacked[r]

        def score(c, peak, r=r, q=q, length=length):
            here = flat.at[:, r, pl.ds(pl.multiple_of(c * 2 * CHUNK, 2 * CHUNK), 2 * CHUNK)]
            pltpu.make_async_copy(
                here, here, sems.at[r, c]
            ).wait()
            s = lax.dot_general(
                q, pairs(r, pl.multiple_of(c * 2 * CHUNK, 2 * CHUNK), 2 * CHUNK), nt, preferred_element_type=F32
            )
            s = jnp.where(place < 2 * (length - c * CHUNK), s * factor, -jnp.inf)
            s_buf[c] = s
            for t in range(2 * CHUNK // 128):
                peak = jnp.maximum(peak, s[:, t * 128 : (t + 1) * 128])
            return peak

        peak = jnp.max(lax.fori_loop(0, chunks, score, fresh[r]), axis=1, keepdims=True)

        w = jnp.exp(fresh[r] - peak)
        acc[...] = jnp.dot(
            pltpu.roll(w, 1, 1).astype(BF16), new_pairs, preferred_element_type=F32
        )

        def weigh(c, total, r=r, peak=peak):
            moved = []
            for t in range(2 * CHUNK // 128):
                w = jnp.exp(s_buf[c, :, t * 128 : (t + 1) * 128] - peak)
                total = total + w
                moved.append(pltpu.roll(w, 1, 1).astype(BF16))
            acc[...] += jnp.dot(
                jnp.concatenate(moved, axis=1),
                pairs(r, pl.multiple_of(c * 2 * CHUNK, 2 * CHUNK), 2 * CHUNK),
                preferred_element_type=F32,
            )
            return total

        total = jnp.sum(lax.fori_loop(0, chunks, weigh, w), axis=1, keepdims=True)
        for h in range(KV_HEADS):
            here = slice(h * rows, (h + 1) * rows)
            out = acc[here, h * HEAD_SIZE : (h + 1) * HEAD_SIZE] / total[here]
            for g in range(GROUP):
                o32[h * GROUP + g, r * TOKENS : (r + 1) * TOKENS, :] = out[g * TOKENS : (g + 1) * TOKENS]
    out_ref[...] = o32[...].reshape(KV_HEADS * GROUP * REQS * TOKENS, HEAD_SIZE).astype(BF16)


def attention(queries, new_token_pairs, paged_cache_store, page_table, cache_lengths):
    smem = pl.BlockSpec(memory_space=pltpu.SMEM)
    vmem = pl.BlockSpec(memory_space=pltpu.VMEM)
    anywhere = pl.BlockSpec(memory_space=pl.ANY)
    return pl.pallas_call(
        attend,
        out_shape=jax.ShapeDtypeStruct((256, HEAD_SIZE), BF16),
        in_specs=[smem, smem, vmem, anywhere, anywhere],
        out_specs=vmem,
        scratch_shapes=[
            pltpu.VMEM((KV_HEADS, REQS, 2 * MAXLEN, HEAD_SIZE), BF16),
            pltpu.VMEM((KV_HEADS, 128, HEAD_SIZE), BF16),
            pltpu.VMEM((MAXLEN // CHUNK, KV_HEADS * GROUP * TOKENS, 2 * CHUNK), F32),
            pltpu.VMEM((KV_HEADS * GROUP * TOKENS, KV_HEADS * HEAD_SIZE), F32),
            pltpu.VMEM((KV_HEADS * GROUP, REQS * TOKENS, HEAD_SIZE), F32),
            pltpu.SemaphoreType.DMA((REQS, MAXLEN // CHUNK)),
            pltpu.SemaphoreType.DMA((KV_HEADS,)),
        ],
        compiler_params=pltpu.CompilerParams(vmem_limit_bytes=58 << 20),
        name="paged_attention",
    )(page_table, cache_lengths, queries, new_token_pairs, paged_cache_store)


def split(at, size):
    first = next(a for a in LAYOUT if isinstance(at[a], slice))
    half = size[first] // 2
    return first, ({**at, first: pl.ds(0, half)}, {**at, first: pl.ds(half, half)})


class Gather:
    def __init__(self, net, buf, coord, offsets, parts, sems, base):
        self.net, self.buf, self.coord, self.offsets, self.parts = net, buf, coord, offsets, parts
        self.size = {"z": buf.shape[0], "y": buf.shape[2], "x": buf.shape[3]}
        self.send, self.recv, self.fsend, self.frecv = sems
        self.base, self.fbase = base * 36, base * 21
        self.held = [dict(coord) for _ in parts]
        self.pending = [[] for _ in parts]
        self.flying, self.forwards = [], []

    def region(self, at, rows):
        return self.buf.at[at["z"], self.net.core, at["y"], at["x"], pl.ds(*rows)]

    def forward(self, at, rows, slot):
        part = self.region(at, rows)
        slot = self.fbase + slot
        copy = self.net.copy(part, part, self.fsend.at[slot], self.frecv.at[slot], self.net.sibling)
        copy.start()
        self.forwards.append(copy)

    def push(self, p, slot, at, axis, k):
        slot = p * 12 + slot
        block = self.region(at, self.parts[p])
        copy = self.net.copy(
            block, block, self.send.at[self.base + slot], self.recv.at[self.base + slot], self.net.shifted(axis, k)
        )
        copy.start()
        self.flying.append(copy)
        return copy, slot

    def came(self, axis, k):
        return (self.coord[axis] + 4 - k) % 4 if self.size[axis] == 4 else 1 - self.coord[axis]

    def ring(self, p):
        return len(self.offsets[ORDERS[p][2]]) == 3

    def launch(self, p, stage):
        axis = ORDERS[p][stage]
        held = self.held[p]
        if stage == 2 and self.ring(p):
            _, (low, high) = split(held, self.size)
            for slot, at, k in ((6, low, 1), (7, high, 3), (8, high, 1), (9, low, 3)):
                copy, slot = self.push(p, slot, at, axis, k)
                self.pending[p].append((copy, slot, {**at, axis: self.came(axis, k)}, k))
            return
        for k in self.offsets[axis]:
            copy, slot = self.push(p, stage * 3 + k - 1, held, axis, k)
            self.pending[p].append((copy, slot, {**held, axis: self.came(axis, k)}, k))

    def start(self):
        for p in range(3):
            self.launch(p, 0)

    def land(self, p, count):
        arrived, self.pending[p] = self.pending[p][:count], self.pending[p][count:]
        for copy, *_ in arrived:
            copy.wait_recv()
        return arrived

    def step(self, stage):
        for p in range(3):
            arrived = self.land(p, len(self.pending[p]))
            if stage < 2:
                axis = ORDERS[p][stage]
                self.held[p] = {**self.held[p], axis: slice(None)}
                self.launch(p, stage + 1)
            else:
                for slot, (_, _, at, _) in enumerate(arrived):
                    self.forward(at, self.parts[p], p * 7 + 3 + slot)
        if stage == 1:
            for p in range(3):
                self.forward(self.held[p], self.parts[p], p * 7)

    def relay(self):
        landed = []
        for p in range(3):
            if not self.ring(p):
                continue
            axis = ORDERS[p][2]
            arrived = self.land(p, 2)
            for (_, _, at, k), slot in zip(arrived, (10, 11)):
                copy, slot = self.push(p, slot, at, axis, k)
                self.pending[p].append((copy, slot, {**at, axis: self.came(axis, 2)}, k))
            landed.append((p, arrived))
        for p, arrived in landed:
            for slot, (_, _, at, _) in enumerate(arrived):
                self.forward(at, self.parts[p], p * 7 + 1 + slot)

    def finish(self):
        for copy in self.forwards:
            copy.wait_recv()

    def drain(self):
        for copy in self.flying + self.forwards:
            copy.wait_send()
        self.flying = []


class Scatter:
    def __init__(self, net, Q, landing, parts, sems, base):
        self.net, self.Q, self.landing, self.parts = net, Q, landing, parts
        self.send, self.recv = sems
        self.base = base * 36
        self.pending = [[] for _ in parts]
        self.flying = []

    def push(self, p, slot, src, dst, axis, k):
        slot = self.base + p * 12 + slot
        copy = self.net.copy(src, dst, self.send.at[slot], self.recv.at[slot], self.net.shifted(axis, k))
        copy.start()
        self.flying.append(copy)
        self.pending[p].append(copy)

    def part(self, p, at):
        return self.Q.at[at["z"], self.net.core, at["y"], at["x"], pl.ds(*self.parts[p])]

    def first(self, p):
        order = ORDERS[p][::-1]
        axis = order[0]
        whole = {a: (self.net.me[a] if a == axis else slice(None)) for a in LAYOUT}
        return axis, split(whole, {a: 4 for a in LAYOUT})[1], [a for a in LAYOUT if a != axis]

    def start(self, p):
        axis, halves, left = self.first(p)
        rows = pl.ds(*self.parts[p])
        me = self.net.me[axis]
        for slot, half, away, k, land in ((0, 0, 2, 1, 2), (1, 1, 2, 3, 2), (2, 1, 1, 1, 0), (3, 0, 3, 3, 1)):
            at = {**halves[half], axis: (me + away) % 4}
            dst = self.landing[0].at[land, pl.ds(half * 2, 2), :, rows]
            self.push(p, slot, self.part(p, at), dst, axis, k)

    def relay(self):
        for p in range(3):
            axis, halves, left = self.first(p)
            rows = pl.ds(*self.parts[p])
            me = self.net.me[axis]
            arrived, self.pending[p] = self.pending[p][:2], self.pending[p][2:]
            for slot, half, k, land in ((4, 0, 1, 0), (5, 1, 3, 1)):
                arrived[half].wait_recv()
                target = (me + k) % 4

                def add(i, _, half=half, rows=rows, target=target, axis=axis, left=left):
                    where = (half * 2 + i // 4, i % 4)
                    at = {axis: target, **dict(zip(left, where))}
                    got = self.landing[0][2, where[0], where[1], rows].astype(F32)
                    spot = (at["z"], self.net.core, at["y"], at["x"], rows)
                    self.Q[spot] = (self.Q[spot].astype(F32) + got).astype(BF16)
                    return 0

                lax.fori_loop(0, 8, add, 0)
                dst = self.landing[0].at[land, pl.ds(half * 2, 2), :, rows]
                self.push(p, slot, self.part(p, {**halves[half], axis: target}), dst, axis, k)

    def launch(self, p, stage):
        order = ORDERS[p][::-1]
        axis, left = order[stage], order[stage + 1 :]
        me = self.net.me
        for k in (1, 2, 3):
            at = {a: (slice(None) if a in left else me[a]) for a in LAYOUT}
            at[axis] = (me[axis] + k) % 4
            dst = self.landing[stage].at[(k - 1, *(slice(None),) * len(left), pl.ds(*self.parts[p]))]
            self.push(p, 3 + stage * 3 + k - 1, self.part(p, at), dst, axis, k)

    def step(self, stage):
        for p in range(3):
            order = ORDERS[p][::-1]
            left = [a for a in LAYOUT if a in order[stage + 1 :]]
            rows = pl.ds(*self.parts[p])
            me, core, Q = self.net.me, self.net.core, self.Q
            land = self.landing[stage]
            for copy in self.pending[p]:
                copy.wait_recv()
            self.pending[p] = []
            if stage == 2:
                continue

            def add(i, _, left=left, rows=rows, land=land):
                where = (i // 4, i % 4) if stage == 0 else (i,)
                at = {**me, **dict(zip(left, where))}
                total = Q[at["z"], core, at["y"], at["x"], rows].astype(F32)
                for k in range(2 if stage == 0 else 3):
                    got = land[k, where[0], where[1], rows] if stage == 0 else land[k, where[0], rows]
                    total = total + got.astype(F32)
                Q[at["z"], core, at["y"], at["x"], rows] = total.astype(BF16)
                return 0

            lax.fori_loop(0, 16 if stage == 0 else 4, add, 0)
            self.launch(p, stage + 1)

    def drain(self):
        for copy in self.flying:
            copy.wait_send()
        self.flying = []


class Net:
    def __init__(self):
        sec, grp, tp = lax.axis_index("sec"), lax.axis_index("grp"), lax.axis_index("tp")
        self.sec, self.zh, self.core = sec, grp // 2, grp % 2
        self.me = {"z": self.zh * 2 + sec, "y": tp // 4, "x": tp % 4}
        self.sibling = self.device(self.me, 1 - self.core)
        self.partner = self.device({**self.me, "z": self.zh * 2 + (1 - sec)}, self.core)

    def device(self, at, core):
        return (at["z"] % 2, (at["z"] // 2) * 2 + core, at["y"] * 4 + at["x"])

    def shifted(self, axis, k):
        return self.device({**self.me, axis: (self.me[axis] + k) % 4}, self.core)

    def copy(self, src, dst, send, recv, to):
        return pltpu.make_async_remote_copy(src, dst, send, recv, device_id=to, device_id_type=MESH)


def layer(
    attn, residual, gain, w_out, w_gate, w_up, w_down, out_ref,
    A, X, Q, RC, R1, R2, R3, sec_in, sec_out, fin_in, fin_out,
    wo, wg, wu, wd, res, scales, acc_g, acc_u, acc_s, hidden, mixed,
    w_sem, s1, r1, f1s, f1r, cs, cr, xs, xr,
):
    net = Net()
    sec, zh, c, me = net.sec, net.zh, net.core, net.me

    barrier = pltpu.get_barrier_semaphore()
    for axis in LAYOUT:
        for k in (1, 2, 3):
            pl.semaphore_signal(barrier, 1, device_id=net.shifted(axis, k), device_id_type=MESH)
    pl.semaphore_signal(barrier, 1, device_id=net.sibling, device_id_type=MESH)

    half_rows = pl.ds(pl.multiple_of(sec * 256, 256), 256)
    loads = [
        pltpu.make_async_copy(src, dst, w_sem.at[i])
        for i, (src, dst) in enumerate(
            (
                (w_out, wo), (w_gate, wg), (w_up, wu), (w_down, wd),
                (attn, A.at[zh, c, me["y"], me["x"]]), (residual.at[half_rows], res), (gain, scales),
            )
        )
    ]
    for i in (4, 5, 6, 0, 1, 2, 3):
        loads[i].start()
    pl.semaphore_wait(barrier, 10)

    loads[4].wait()
    every = (1, 2, 3)
    rows_gather = Gather(
        net, A, {"z": zh, "y": me["y"], "x": me["x"]}, {"z": (2,), "y": every, "x": every},
        PARTS, (s1, r1, f1s, f1r), 0,
    )
    rows_gather.start()

    def scale_weights():
        for i in (1, 2, 6):
            loads[i].wait()

        def scale(i, _):
            cols = pl.ds(pl.multiple_of(i * 512, 512), 512)
            g = scales[:, cols]
            wg[:, cols] = (wg[:, cols].astype(F32) * g).astype(BF16)
            wu[:, cols] = (wu[:, cols].astype(F32) * g).astype(BF16)
            return 0

        lax.fori_loop(0, D // 512, scale, 0)

    rows_gather.step(0)
    rows_gather.step(1)
    rows_gather.relay()
    rows_gather.step(2)

    loads[0].wait()

    def project(core):
        total = jnp.zeros((512, 256), F32)
        for j in range(0, 16, 2):
            lhs = jnp.concatenate(
                [A[:, core, :, :, (j + t) * 16 : (j + t + 1) * 16, :].reshape(512, 128) for t in range(2)], axis=1
            )
            rhs = jnp.concatenate(
                [
                    jnp.concatenate(
                        [wo[(2 * (j + t) + u) * 128 : (2 * (j + t) + u + 1) * 128, :] for u in range(2)], axis=1
                    )
                    for t in range(2)
                ],
                axis=0,
            )
            total = total + jnp.dot(lhs, rhs, preferred_element_type=F32)
        total = total.reshape(32, 2, 8, 256)
        mixed[:, core] = (total[:, 0, :, :128] + total[:, 1, :, 128:]).reshape(2, 128, 128)

    project(c)
    rows_gather.finish()
    project(1 - c)

    sec_out[...] = mixed[1 - sec].reshape(256, 128).astype(BF16)
    swap = net.copy(sec_out, sec_in, xs.at[0], xr.at[0], net.partner)
    swap.start()
    loads[5].wait()
    own = res[...].astype(F32)
    swap.wait_recv()
    X[me["z"], c, me["y"], me["x"]] = (
        own + (mixed[sec].reshape(256, 128) + sec_in[...].astype(F32))
    ).astype(BF16)

    gathers = [
        Gather(
            net, X, me, {"z": every, "y": every, "x": every}, HALF_PARTS[h], (s1, r1, f1s, f1r), h + 1
        )
        for h in range(2)
    ]
    scatters = [Scatter(net, Q, (R1, R2, R3), HALF_PARTS[h], (s1, r1), h) for h in range(2)]

    def ffn_in(h, core, first):
        rows = pl.ds(h * HALF, HALF)
        if first:
            acc_g[...] = jnp.zeros_like(acc_g)
            acc_u[...] = jnp.zeros_like(acc_u)
            acc_s[...] = jnp.zeros_like(acc_s)

        def body(hi, _):
            cols = pl.ds(pl.multiple_of((hi * 2 + core) * 2048, 2048), 2048)
            halves = []
            for lo in range(2):
                blocks = [X[hi * 2 + lo, core, b // 4, b % 4, rows] for b in range(16)]
                squares = acc_s[lo * HALF : (lo + 1) * HALF]
                for b in blocks:
                    wide = b.astype(F32)
                    squares = squares + wide * wide
                acc_s[lo * HALF : (lo + 1) * HALF] = squares
                halves.append(jnp.concatenate(blocks, axis=1))
            lhs = jnp.concatenate(halves, axis=0)
            nt = (((1,), (1,)), ((), ()))
            acc_g[...] += lax.dot_general(lhs, wg[:, cols], nt, preferred_element_type=F32)
            acc_u[...] += lax.dot_general(lhs, wu[:, cols], nt, preferred_element_type=F32)
            return 0

        lax.fori_loop(0, 2, body, 0)

    def activate():
        inv = lax.rsqrt(jnp.sum(acc_s[...], axis=1, keepdims=True) / D + EPS)
        gate = acc_g[...] * inv
        hidden[...] = (gate / (1.0 + jnp.exp(-gate)) * (acc_u[...] * inv)).astype(BF16)

    def core_copy(h, p):
        rows = pl.ds(*HALF_PARTS[h][p])
        return net.copy(
            Q.at[:, 1 - c, :, :, rows], RC.at[:, :, :, rows], cs.at[h * 3 + p], cr.at[h * 3 + p], net.sibling
        )

    def ffn_out(h):
        rows = pl.ds(h * HALF, HALF)

        def tile(core, hi):
            cols = pl.ds(pl.multiple_of((hi * 2 + core) * 2048, 2048), 2048)
            part = jnp.dot(hidden[...], wd[:, cols], preferred_element_type=F32)
            for lo in range(2):
                for y in range(4):
                    for x in range(4):
                        Q[hi * 2 + lo, core, y, x, rows] = part[
                            lo * HALF : (lo + 1) * HALF, (y * 4 + x) * 128 : (y * 4 + x + 1) * 128
                        ].astype(BF16)

        for hi in range(2):
            tile(1 - c, hi)
        swaps = [core_copy(h, p) for p in range(3)]
        for copy in swaps:
            copy.start()
        for hi in range(2):
            tile(c, hi)
        for p in range(3):
            here = pl.ds(*HALF_PARTS[h][p])
            swaps[p].wait_recv()

            def add_sibling(i, _, here=here):
                z, y = i // 4, i % 4
                for x in range(4):
                    Q[z, c, y, x, here] = (Q[z, c, y, x, here].astype(F32) + RC[z, y, x, here].astype(F32)).astype(
                        BF16
                    )
                return 0

            lax.fori_loop(0, 16, add_sibling, 0)
            scatters[h].start(p)
        return swaps

    def close(h):
        rows = pl.ds(h * HALF, HALF)
        total = X[me["z"], c, me["y"], me["x"], rows].astype(F32)
        ffn = Q[me["z"], c, me["y"], me["x"], rows].astype(F32)
        for k in range(3):
            ffn = ffn + R3[k, rows].astype(F32)
        done = (total + ffn).astype(BF16)
        fin_out[rows] = done
        last = net.copy(fin_out.at[rows], fin_in.at[rows], xs.at[1 + h], xr.at[1 + h], net.partner)
        last.start()
        out_ref[pl.ds(pl.multiple_of(sec * 256 + h * HALF, HALF), HALF), :] = done
        return last

    g0, g1 = gathers
    t0, t1 = scatters
    g0.start()
    rows_gather.drain()
    g0.step(0)
    g1.start()
    g0.step(1)
    g1.step(0)
    g0.relay()
    g1.step(1)
    scale_weights()
    g0.step(2)
    ffn_in(0, c, True)
    g0.finish()
    ffn_in(0, 1 - c, False)
    g1.relay()
    activate()
    loads[3].wait()
    swaps = ffn_out(0)
    g1.step(2)
    ffn_in(1, c, True)
    g1.finish()
    t0.relay()
    ffn_in(1, 1 - c, False)
    activate()
    g0.drain()
    swaps += ffn_out(1)
    t0.step(0)
    t1.relay()
    g1.drain()
    for copy in swaps:
        copy.wait_send()
    t0.step(1)
    t1.step(0)
    t0.step(2)
    last0 = close(0)
    t0.drain()
    t1.drain()
    t1.step(1)
    t1.step(2)
    last1 = close(1)
    swap.wait_send()
    t1.drain()
    last0.wait()
    last1.wait()
    out_ref[pl.ds(pl.multiple_of((1 - sec) * 256, 256), 256), :] = fin_in[...]


def rest(attn, residual, gain, w_out, w_gate, w_up, w_down):
    vmem = pl.BlockSpec(memory_space=pltpu.VMEM)
    anywhere = pl.BlockSpec(memory_space=pl.ANY)
    dma = pltpu.SemaphoreType.DMA
    return pl.pallas_call(
        layer,
        out_shape=jax.ShapeDtypeStruct((512, 128), BF16),
        in_specs=[anywhere] * 7,
        out_specs=vmem,
        scratch_shapes=[
            pltpu.VMEM((2, 2, 4, 4, 256, 128), BF16),
            pltpu.VMEM((4, 2, 4, 4, 256, 128), BF16),
            pltpu.VMEM((4, 2, 4, 4, 256, 128), BF16),
            pltpu.VMEM((4, 4, 4, 256, 128), BF16),
            pltpu.VMEM((3, 4, 4, 256, 128), BF16),
            pltpu.VMEM((3, 4, 256, 128), BF16),
            pltpu.VMEM((3, 256, 128), BF16),
            pltpu.VMEM((256, 128), BF16),
            pltpu.VMEM((256, 128), BF16),
            pltpu.VMEM((256, 128), BF16),
            pltpu.VMEM((256, 128), BF16),
            pltpu.VMEM(w_out.shape, BF16),
            pltpu.VMEM(w_gate.shape, BF16),
            pltpu.VMEM(w_up.shape, BF16),
            pltpu.VMEM(w_down.shape, BF16),
            pltpu.VMEM((256, 128), BF16),
            pltpu.VMEM((1, D), F32),
            pltpu.VMEM((256, w_gate.shape[0]), F32),
            pltpu.VMEM((256, w_gate.shape[0]), F32),
            pltpu.VMEM((256, 128), F32),
            pltpu.VMEM((256, w_gate.shape[0]), BF16),
            pltpu.VMEM((2, 2, 128, 128), F32),
            dma((7,)),
            dma((108,)), dma((108,)), dma((63,)), dma((63,)),
            dma((6,)), dma((6,)),
            dma((3,)), dma((3,)),
        ],
        compiler_params=pltpu.CompilerParams(collective_id=0, has_side_effects=True, vmem_limit_bytes=60 << 20),
        name="layer_rest",
    )(attn, residual, gain, w_out, w_gate, w_up, w_down)


def per_device(
    queries, new_token_pairs, paged_cache_store, page_table, cache_lengths,
    out_weight, residual, norm_gain, gate_weight, up_weight, down_weight,
):
    attn = attention(queries, new_token_pairs, paged_cache_store, page_table, cache_lengths)
    return rest(attn, residual, norm_gain.reshape(1, D), out_weight, gate_weight, up_weight, down_weight)


def solution(mesh):
    in_specs = (
        P(("grp", "tp"), None, "sec"),
        P(("grp", "tp"), None, None, "sec"),
        P(("grp", "tp"), None, None, "sec"),
        P(("grp", "tp"), None),
        P(("grp", "tp")),
        P("sec", ("grp", "tp")),
        P(None, ("grp", "tp")),
        P(),
        P(("sec", "grp", "tp"), None),
        P(("sec", "grp", "tp"), None),
        P(("sec", "grp", "tp"), None),
    )
    out_specs = P(None, ("grp", "tp"))
    return jax.shard_map(
        per_device, mesh=mesh, in_specs=in_specs, out_specs=out_specs, check_vma=False
    )
```

```python
import functools
import math

import jax
import jax.numpy as jnp
from jax import lax
from jax.experimental import pallas as pl
from jax.experimental.pallas import tpu as pltpu
from jax.sharding import PartitionSpec as P

D = 8192
HEAD_SIZE = 128
EPS = 1e-05
MESH = pl.DeviceIdType.MESH
F32 = jnp.float32
BF16 = jnp.bfloat16

PAGE = 64
CHUNK_PAGES = 8
CHUNK = PAGE * CHUNK_PAGES
MAXLEN = 3072
REQS = 2
KV_HEADS = 4
GROUP = 8
TOKENS = 4
NEW_ROWS = REQS * TOKENS * 2

PARTS = ((0, 64), (64, 96), (160, 96))
HALF_PARTS = (((0, 48), (48, 48), (96, 32)), ((128, 32), (160, 48), (208, 48)))
HALF = 128
ORDERS = (("x", "y", "z"), ("y", "z", "x"), ("z", "x", "y"))
LAYOUT = ("z", "y", "x")


def attend(table, lengths, q_ref, new_ref, kv_ref, out_ref, flat, new_flat, s_buf, acc, o32, sems, new_sems):
    kv_rows = kv_ref.reshape(kv_ref.shape[0], 2 * PAGE, KV_HEADS * HEAD_SIZE)
    new_rows = new_ref.reshape(NEW_ROWS, KV_HEADS * HEAD_SIZE)
    factor = 1.0 / math.sqrt(HEAD_SIZE)
    rows = GROUP * TOKENS
    queries = KV_HEADS * rows
    nt = (((1,), (1,)), ((), ()))

    new_copies = []
    new_flat[:, pl.ds(NEW_ROWS, 128 - NEW_ROWS), :] = jnp.zeros((KV_HEADS, 128 - NEW_ROWS, HEAD_SIZE), BF16)
    for h in range(KV_HEADS):
        copy = pltpu.make_async_copy(
            new_rows.at[:, pl.ds(h * HEAD_SIZE, HEAD_SIZE)], new_flat.at[h, pl.ds(0, NEW_ROWS)], new_sems.at[h]
        )
        copy.start()
        new_copies.append(copy)

    for r in range(REQS):
        chunks = (lengths[r] + CHUNK - 1) // CHUNK

        def start(p, _, r=r):
            page = table[r, p]
            for h in range(KV_HEADS):
                pltpu.make_async_copy(
                    kv_rows.at[page, :, pl.ds(h * HEAD_SIZE, HEAD_SIZE)],
                    flat.at[h, r, pl.ds(pl.multiple_of(p * 2 * PAGE, 2 * PAGE), 2 * PAGE)],
                    sems.at[r, p // CHUNK_PAGES],
                ).start()
            return 0

        lax.fori_loop(0, chunks * CHUNK_PAGES, start, 0)

    stacked = []
    for r in range(REQS):
        wide = q_ref[r].astype(F32)
        blocks = []
        for h in range(KV_HEADS):
            q = jnp.concatenate(
                [wide[:, (h * GROUP + g) * HEAD_SIZE : (h * GROUP + g + 1) * HEAD_SIZE] for g in range(GROUP)], axis=0
            ).astype(BF16)
            zero = jnp.zeros_like(q)
            blocks.append(jnp.concatenate([q if k == h else zero for k in range(KV_HEADS)], axis=1))
        stacked.append(jnp.concatenate(blocks, axis=0))

    def pairs(r, first, count):
        return jnp.concatenate([flat[h, r, pl.ds(first, count), :] for h in range(KV_HEADS)], axis=1)

    col = lax.broadcasted_iota(jnp.int32, (queries, 128), 1)
    row = lax.broadcasted_iota(jnp.int32, (queries, 128), 0)
    wide_col = lax.broadcasted_iota(jnp.int32, (8, 2 * CHUNK), 1)
    place = jnp.where(wide_col % 2 == 0, wide_col, 2 * MAXLEN)[:1]

    for copy in new_copies:
        copy.wait()
    new_pairs = jnp.concatenate([new_flat[h] for h in range(KV_HEADS)], axis=1)
    fresh = []
    for r in range(REQS):
        s = lax.dot_general(stacked[r], new_pairs, nt, preferred_element_type=F32)
        token = (col - r * 2 * TOKENS) // 2
        live = (col % 2 == 0) & (col >= r * 2 * TOKENS) & (token <= row % TOKENS)
        fresh.append(jnp.where(live, s * factor, -jnp.inf))

    for r in range(REQS):
        length = lengths[r]
        chunks = (length + CHUNK - 1) // CHUNK
        q = stacked[r]

        def score(c, peak, r=r, q=q, length=length):
            here = flat.at[:, r, pl.ds(pl.multiple_of(c * 2 * CHUNK, 2 * CHUNK), 2 * CHUNK)]
            pltpu.make_async_copy(
                here, here, sems.at[r, c]
            ).wait()
            s = lax.dot_general(
                q, pairs(r, pl.multiple_of(c * 2 * CHUNK, 2 * CHUNK), 2 * CHUNK), nt, preferred_element_type=F32
            )
            s = jnp.where(place < 2 * (length - c * CHUNK), s * factor, -jnp.inf)
            s_buf[c] = s
            for t in range(2 * CHUNK // 128):
                peak = jnp.maximum(peak, s[:, t * 128 : (t + 1) * 128])
            return peak

        peak = jnp.max(lax.fori_loop(0, chunks, score, fresh[r]), axis=1, keepdims=True)

        w = jnp.exp(fresh[r] - peak)
        acc[...] = jnp.dot(
            pltpu.roll(w, 1, 1).astype(BF16), new_pairs, preferred_element_type=F32
        )

        def weigh(c, total, r=r, peak=peak):
            moved = []
            for t in range(2 * CHUNK // 128):
                w = jnp.exp(s_buf[c, :, t * 128 : (t + 1) * 128] - peak)
                total = total + w
                moved.append(pltpu.roll(w, 1, 1).astype(BF16))
            acc[...] += jnp.dot(
                jnp.concatenate(moved, axis=1),
                pairs(r, pl.multiple_of(c * 2 * CHUNK, 2 * CHUNK), 2 * CHUNK),
                preferred_element_type=F32,
            )
            return total

        total = jnp.sum(lax.fori_loop(0, chunks, weigh, w), axis=1, keepdims=True)
        for h in range(KV_HEADS):
            here = slice(h * rows, (h + 1) * rows)
            out = acc[here, h * HEAD_SIZE : (h + 1) * HEAD_SIZE] / total[here]
            for g in range(GROUP):
                o32[h * GROUP + g, r * TOKENS : (r + 1) * TOKENS, :] = out[g * TOKENS : (g + 1) * TOKENS]
    out_ref[...] = o32[...].reshape(KV_HEADS * GROUP * REQS * TOKENS, HEAD_SIZE).astype(BF16)


def attention(queries, new_token_pairs, paged_cache_store, page_table, cache_lengths):
    smem = pl.BlockSpec(memory_space=pltpu.SMEM)
    vmem = pl.BlockSpec(memory_space=pltpu.VMEM)
    anywhere = pl.BlockSpec(memory_space=pl.ANY)
    return pl.pallas_call(
        attend,
        out_shape=jax.ShapeDtypeStruct((256, HEAD_SIZE), BF16),
        in_specs=[smem, smem, vmem, anywhere, anywhere],
        out_specs=vmem,
        scratch_shapes=[
            pltpu.VMEM((KV_HEADS, REQS, 2 * MAXLEN, HEAD_SIZE), BF16),
            pltpu.VMEM((KV_HEADS, 128, HEAD_SIZE), BF16),
            pltpu.VMEM((MAXLEN // CHUNK, KV_HEADS * GROUP * TOKENS, 2 * CHUNK), F32),
            pltpu.VMEM((KV_HEADS * GROUP * TOKENS, KV_HEADS * HEAD_SIZE), F32),
            pltpu.VMEM((KV_HEADS * GROUP, REQS * TOKENS, HEAD_SIZE), F32),
            pltpu.SemaphoreType.DMA((REQS, MAXLEN // CHUNK)),
            pltpu.SemaphoreType.DMA((KV_HEADS,)),
        ],
        compiler_params=pltpu.CompilerParams(vmem_limit_bytes=58 << 20),
        name="paged_attention",
    )(page_table, cache_lengths, queries, new_token_pairs, paged_cache_store)


def split(at, size):
    first = next(a for a in LAYOUT if isinstance(at[a], slice))
    half = size[first] // 2
    return first, ({**at, first: pl.ds(0, half)}, {**at, first: pl.ds(half, half)})


def drain(buf, tiles, sem):
    blocks = buf.reshape(-1, 256, 128)
    rows = next(r for r in range(256, 0, -16) if tiles * 16 % r == 0 and tiles * 16 // r <= blocks.shape[0])
    bulk = blocks.at[pl.ds(0, tiles * 16 // rows), pl.ds(0, rows)]
    pltpu.make_async_copy(bulk, bulk, sem).wait()


class Gather:
    def __init__(self, net, buf, coord, offsets, parts, sems, base):
        self.net, self.buf, self.coord, self.offsets, self.parts = net, buf, coord, offsets, parts
        self.size = {"z": buf.shape[0], "y": buf.shape[2], "x": buf.shape[3]}
        self.send, self.recv, self.fsend, self.frecv = sems
        self.turn, self.base, self.fbase = base, base * 36, base * 21
        self.sent = self.passed = 0
        self.held = [dict(coord) for _ in parts]
        self.pending = [[] for _ in parts]
        self.forwards = []

    def region(self, at, rows):
        return self.buf.at[at["z"], self.net.core, at["y"], at["x"], pl.ds(*rows)]

    def forward(self, at, rows, slot):
        part = self.region(at, rows)
        slot = self.fbase + slot
        copy = self.net.copy(part, part, self.fsend.at[self.turn], self.frecv.at[slot], self.net.sibling)
        copy.start()
        self.passed += math.prod(part.shape) // 2048
        self.forwards.append(copy)

    def push(self, p, slot, at, axis, k):
        slot = p * 12 + slot
        block = self.region(at, self.parts[p])
        copy = self.net.copy(
            block, block, self.send.at[self.turn], self.recv.at[self.base + slot], self.net.shifted(axis, k)
        )
        copy.start()
        self.sent += math.prod(block.shape) // 2048
        return copy, slot

    def came(self, axis, k):
        return (self.coord[axis] + 4 - k) % 4 if self.size[axis] == 4 else 1 - self.coord[axis]

    def ring(self, p):
        return len(self.offsets[ORDERS[p][2]]) == 3

    def launch(self, p, stage):
        axis = ORDERS[p][stage]
        held = self.held[p]
        if stage == 2 and self.ring(p):
            _, (low, high) = split(held, self.size)
            for slot, at, k in ((6, low, 1), (7, high, 3), (8, high, 1), (9, low, 3)):
                copy, slot = self.push(p, slot, at, axis, k)
                self.pending[p].append((copy, slot, {**at, axis: self.came(axis, k)}, k))
            return
        for k in self.offsets[axis]:
            copy, slot = self.push(p, stage * 3 + k - 1, held, axis, k)
            self.pending[p].append((copy, slot, {**held, axis: self.came(axis, k)}, k))

    def start(self):
        for p in range(3):
            self.launch(p, 0)

    def land(self, p, count):
        arrived, self.pending[p] = self.pending[p][:count], self.pending[p][count:]
        for copy, *_ in arrived:
            copy.wait_recv()
        return arrived

    def step(self, stage):
        for p in range(3):
            arrived = self.land(p, len(self.pending[p]))
            if stage < 2:
                axis = ORDERS[p][stage]
                self.held[p] = {**self.held[p], axis: slice(None)}
                self.launch(p, stage + 1)
            else:
                for slot, (_, _, at, _) in enumerate(arrived):
                    self.forward(at, self.parts[p], p * 7 + 3 + slot)
        if stage == 1:
            for p in range(3):
                self.forward(self.held[p], self.parts[p], p * 7)

    def relay(self):
        landed = []
        for p in range(3):
            if not self.ring(p):
                continue
            axis = ORDERS[p][2]
            arrived = self.land(p, 2)
            for (_, _, at, k), slot in zip(arrived, (10, 11)):
                copy, slot = self.push(p, slot, at, axis, k)
                self.pending[p].append((copy, slot, {**at, axis: self.came(axis, 2)}, k))
            landed.append((p, arrived))
        for p, arrived in landed:
            for slot, (_, _, at, _) in enumerate(arrived):
                self.forward(at, self.parts[p], p * 7 + 1 + slot)

    def finish(self):
        for copy in self.forwards:
            copy.wait_recv()

    def drain(self):
        drain(self.buf, self.sent, self.send.at[self.turn])
        drain(self.buf, self.passed, self.fsend.at[self.turn])


class Scatter:
    def __init__(self, net, Q, landing, parts, sems, base):
        self.net, self.Q, self.landing, self.parts = net, Q, landing, parts
        self.send, self.recv = sems
        self.turn, self.base = base, base * 36
        self.pending = [[] for _ in parts]
        self.sent = 0

    def push(self, p, slot, src, dst, axis, k):
        slot = self.base + p * 12 + slot
        copy = self.net.copy(src, dst, self.send.at[3 + self.turn], self.recv.at[slot], self.net.shifted(axis, k))
        copy.start()
        self.sent += math.prod(src.shape) // 2048
        self.pending[p].append(copy)

    def part(self, p, at):
        return self.Q.at[at["z"], self.net.core, at["y"], at["x"], pl.ds(*self.parts[p])]

    def first(self, p):
        order = ORDERS[p][::-1]
        axis = order[0]
        whole = {a: (self.net.me[a] if a == axis else slice(None)) for a in LAYOUT}
        return axis, split(whole, {a: 4 for a in LAYOUT})[1], [a for a in LAYOUT if a != axis]

    def start(self, p):
        axis, halves, left = self.first(p)
        rows = pl.ds(*self.parts[p])
        me = self.net.me[axis]
        for slot, half, away, k, land in ((0, 0, 2, 1, 2), (1, 1, 2, 3, 2), (2, 1, 1, 1, 0), (3, 0, 3, 3, 1)):
            at = {**halves[half], axis: (me + away) % 4}
            dst = self.landing[0].at[land, pl.ds(half * 2, 2), :, rows]
            self.push(p, slot, self.part(p, at), dst, axis, k)

    def relay(self):
        for p in range(3):
            axis, halves, left = self.first(p)
            rows = pl.ds(*self.parts[p])
            me = self.net.me[axis]
            arrived, self.pending[p] = self.pending[p][:2], self.pending[p][2:]
            for slot, half, k, land in ((4, 0, 1, 0), (5, 1, 3, 1)):
                arrived[half].wait_recv()
                target = (me + k) % 4

                def add(i, _, half=half, rows=rows, target=target, axis=axis, left=left):
                    where = (half * 2 + i // 4, i % 4)
                    at = {axis: target, **dict(zip(left, where))}
                    got = self.landing[0][2, where[0], where[1], rows].astype(F32)
                    spot = (at["z"], self.net.core, at["y"], at["x"], rows)
                    self.Q[spot] = (self.Q[spot].astype(F32) + got).astype(BF16)
                    return 0

                lax.fori_loop(0, 8, add, 0)
                dst = self.landing[0].at[land, pl.ds(half * 2, 2), :, rows]
                self.push(p, slot, self.part(p, {**halves[half], axis: target}), dst, axis, k)

    def launch(self, p, stage):
        order = ORDERS[p][::-1]
        axis, left = order[stage], order[stage + 1 :]
        me = self.net.me
        for k in (1, 2, 3):
            at = {a: (slice(None) if a in left else me[a]) for a in LAYOUT}
            at[axis] = (me[axis] + k) % 4
            dst = self.landing[stage].at[(k - 1, *(slice(None),) * len(left), pl.ds(*self.parts[p]))]
            self.push(p, 3 + stage * 3 + k - 1, self.part(p, at), dst, axis, k)

    def step(self, stage):
        for p in range(3):
            order = ORDERS[p][::-1]
            left = [a for a in LAYOUT if a in order[stage + 1 :]]
            rows = pl.ds(*self.parts[p])
            me, core, Q = self.net.me, self.net.core, self.Q
            land = self.landing[stage]
            for copy in self.pending[p]:
                copy.wait_recv()
            self.pending[p] = []
            if stage == 2:
                continue

            def add(i, _, left=left, rows=rows, land=land):
                where = (i // 4, i % 4) if stage == 0 else (i,)
                at = {**me, **dict(zip(left, where))}
                total = Q[at["z"], core, at["y"], at["x"], rows].astype(F32)
                for k in range(2 if stage == 0 else 3):
                    got = land[k, where[0], where[1], rows] if stage == 0 else land[k, where[0], rows]
                    total = total + got.astype(F32)
                Q[at["z"], core, at["y"], at["x"], rows] = total.astype(BF16)
                return 0

            lax.fori_loop(0, 16 if stage == 0 else 4, add, 0)
            self.launch(p, stage + 1)

    def drain(self):
        drain(self.Q, self.sent, self.send.at[3 + self.turn])


class Net:
    def __init__(self):
        sec, grp, tp = lax.axis_index("sec"), lax.axis_index("grp"), lax.axis_index("tp")
        self.sec, self.zh, self.core = sec, grp // 2, grp % 2
        self.me = {"z": self.zh * 2 + sec, "y": tp // 4, "x": tp % 4}
        self.sibling = self.device(self.me, 1 - self.core)
        self.partner = self.device({**self.me, "z": self.zh * 2 + (1 - sec)}, self.core)

    def device(self, at, core):
        return (at["z"] % 2, (at["z"] // 2) * 2 + core, at["y"] * 4 + at["x"])

    def shifted(self, axis, k):
        return self.device({**self.me, axis: (self.me[axis] + k) % 4}, self.core)

    def copy(self, src, dst, send, recv, to):
        return pltpu.make_async_remote_copy(src, dst, send, recv, device_id=to, device_id_type=MESH)


def layer(
    attn, residual, gain, w_out, w_gate, w_up, w_down, out_ref,
    A, X, Q, RC, R1, R2, R3, sec_in, sec_out, fin_in, fin_out,
    wo, wg, wu, wd, res, scales, acc_g, acc_u, acc_s, hidden, mixed,
    w_sem, s1, r1, f1s, f1r, cs, cr, xs, xr,
):
    net = Net()
    sec, zh, c, me = net.sec, net.zh, net.core, net.me

    barrier = pltpu.get_barrier_semaphore()
    for axis in LAYOUT:
        for k in (1, 2, 3):
            pl.semaphore_signal(barrier, 1, device_id=net.shifted(axis, k), device_id_type=MESH)
    pl.semaphore_signal(barrier, 1, device_id=net.sibling, device_id_type=MESH)

    half_rows = pl.ds(pl.multiple_of(sec * 256, 256), 256)
    loads = [
        pltpu.make_async_copy(src, dst, w_sem.at[i])
        for i, (src, dst) in enumerate(
            (
                (w_out, wo), (w_gate, wg), (w_up, wu), (w_down, wd),
                (attn, A.at[zh, c, me["y"], me["x"]]), (residual.at[half_rows], res), (gain, scales),
            )
        )
    ]
    for i in (4, 5, 6, 0, 1, 2, 3):
        loads[i].start()
    pl.semaphore_wait(barrier, 10)

    loads[4].wait()
    every = (1, 2, 3)
    rows_gather = Gather(
        net, A, {"z": zh, "y": me["y"], "x": me["x"]}, {"z": (2,), "y": every, "x": every},
        PARTS, (s1, r1, f1s, f1r), 0,
    )
    rows_gather.start()

    def scale_weights():
        for i in (1, 2, 6):
            loads[i].wait()

        def scale(i, _):
            cols = pl.ds(pl.multiple_of(i * 512, 512), 512)
            g = scales[:, cols]
            wg[:, cols] = (wg[:, cols].astype(F32) * g).astype(BF16)
            wu[:, cols] = (wu[:, cols].astype(F32) * g).astype(BF16)
            return 0

        lax.fori_loop(0, D // 512, scale, 0)

    rows_gather.step(0)
    rows_gather.step(1)
    rows_gather.relay()
    rows_gather.step(2)

    loads[0].wait()

    def project(core):
        total = jnp.zeros((512, 256), F32)
        for j in range(0, 16, 2):
            lhs = jnp.concatenate(
                [A[:, core, :, :, (j + t) * 16 : (j + t + 1) * 16, :].reshape(512, 128) for t in range(2)], axis=1
            )
            rhs = jnp.concatenate(
                [
                    jnp.concatenate(
                        [wo[(2 * (j + t) + u) * 128 : (2 * (j + t) + u + 1) * 128, :] for u in range(2)], axis=1
                    )
                    for t in range(2)
                ],
                axis=0,
            )
            total = total + jnp.dot(lhs, rhs, preferred_element_type=F32)
        total = total.reshape(32, 2, 8, 256)
        mixed[:, core] = (total[:, 0, :, :128] + total[:, 1, :, 128:]).reshape(2, 128, 128)

    project(c)
    rows_gather.finish()
    project(1 - c)

    sec_out[...] = mixed[1 - sec].reshape(256, 128).astype(BF16)
    swap = net.copy(sec_out, sec_in, xs.at[0], xr.at[0], net.partner)
    swap.start()
    loads[5].wait()
    own = res[...].astype(F32)
    swap.wait_recv()
    X[me["z"], c, me["y"], me["x"]] = (
        own + (mixed[sec].reshape(256, 128) + sec_in[...].astype(F32))
    ).astype(BF16)

    gathers = [
        Gather(
            net, X, me, {"z": every, "y": every, "x": every}, HALF_PARTS[h], (s1, r1, f1s, f1r), h + 1
        )
        for h in range(2)
    ]
    scatters = [Scatter(net, Q, (R1, R2, R3), HALF_PARTS[h], (s1, r1), h) for h in range(2)]

    def ffn_in(h, core, first):
        rows = pl.ds(h * HALF, HALF)
        if first:
            acc_g[...] = jnp.zeros_like(acc_g)
            acc_u[...] = jnp.zeros_like(acc_u)
            acc_s[...] = jnp.zeros_like(acc_s)

        def body(hi, _):
            cols = pl.ds(pl.multiple_of((hi * 2 + core) * 2048, 2048), 2048)
            halves = []
            for lo in range(2):
                blocks = [X[hi * 2 + lo, core, b // 4, b % 4, rows] for b in range(16)]
                squares = acc_s[lo * HALF : (lo + 1) * HALF]
                for b in blocks:
                    wide = b.astype(F32)
                    squares = squares + wide * wide
                acc_s[lo * HALF : (lo + 1) * HALF] = squares
                halves.append(jnp.concatenate(blocks, axis=1))
            lhs = jnp.concatenate(halves, axis=0)
            nt = (((1,), (1,)), ((), ()))
            acc_g[...] += lax.dot_general(lhs, wg[:, cols], nt, preferred_element_type=F32)
            acc_u[...] += lax.dot_general(lhs, wu[:, cols], nt, preferred_element_type=F32)
            return 0

        lax.fori_loop(0, 2, body, 0)

    def activate():
        inv = lax.rsqrt(jnp.sum(acc_s[...], axis=1, keepdims=True) / D + EPS)
        gate = acc_g[...] * inv
        hidden[...] = (gate / (1.0 + jnp.exp(-gate)) * (acc_u[...] * inv)).astype(BF16)

    def core_copy(h, p):
        rows = pl.ds(*HALF_PARTS[h][p])
        return net.copy(
            Q.at[:, 1 - c, :, :, rows], RC.at[:, :, :, rows], cs.at[h * 3 + p], cr.at[h * 3 + p], net.sibling
        )

    def ffn_out(h):
        rows = pl.ds(h * HALF, HALF)

        def tile(core, hi):
            cols = pl.ds(pl.multiple_of((hi * 2 + core) * 2048, 2048), 2048)
            part = jnp.dot(hidden[...], wd[:, cols], preferred_element_type=F32)
            for lo in range(2):
                for y in range(4):
                    for x in range(4):
                        Q[hi * 2 + lo, core, y, x, rows] = part[
                            lo * HALF : (lo + 1) * HALF, (y * 4 + x) * 128 : (y * 4 + x + 1) * 128
                        ].astype(BF16)

        for hi in range(2):
            tile(1 - c, hi)
        swaps = [core_copy(h, p) for p in range(3)]
        for copy in swaps:
            copy.start()
        for hi in range(2):
            tile(c, hi)
        for p in range(3):
            here = pl.ds(*HALF_PARTS[h][p])
            swaps[p].wait_recv()

            def add_sibling(i, _, here=here):
                z, y = i // 4, i % 4
                for x in range(4):
                    Q[z, c, y, x, here] = (Q[z, c, y, x, here].astype(F32) + RC[z, y, x, here].astype(F32)).astype(
                        BF16
                    )
                return 0

            lax.fori_loop(0, 16, add_sibling, 0)
            scatters[h].start(p)
        return swaps

    def close(h):
        rows = pl.ds(h * HALF, HALF)
        total = X[me["z"], c, me["y"], me["x"], rows].astype(F32)
        ffn = Q[me["z"], c, me["y"], me["x"], rows].astype(F32)
        for k in range(3):
            ffn = ffn + R3[k, rows].astype(F32)
        done = (total + ffn).astype(BF16)
        fin_out[rows] = done
        last = net.copy(fin_out.at[rows], fin_in.at[rows], xs.at[1 + h], xr.at[1 + h], net.partner)
        last.start()
        out_ref[pl.ds(pl.multiple_of(sec * 256 + h * HALF, HALF), HALF), :] = done
        return last

    g0, g1 = gathers
    t0, t1 = scatters
    g0.start()
    rows_gather.drain()
    g0.step(0)
    g1.start()
    g0.step(1)
    g1.step(0)
    g0.relay()
    g1.step(1)
    scale_weights()
    g0.step(2)
    ffn_in(0, c, True)
    g0.finish()
    ffn_in(0, 1 - c, False)
    g1.relay()
    activate()
    loads[3].wait()
    swaps = ffn_out(0)
    g1.step(2)
    ffn_in(1, c, True)
    g1.finish()
    t0.relay()
    ffn_in(1, 1 - c, False)
    activate()
    g0.drain()
    swaps += ffn_out(1)
    t0.step(0)
    t1.relay()
    g1.drain()
    for copy in swaps:
        copy.wait_send()
    t0.step(1)
    t1.step(0)
    t0.step(2)
    last0 = close(0)
    t0.drain()
    t1.step(1)
    t1.step(2)
    last1 = close(1)
    swap.wait_send()
    t1.drain()
    last0.wait()
    last1.wait()
    out_ref[pl.ds(pl.multiple_of((1 - sec) * 256, 256), 256), :] = fin_in[...]


def rest(attn, residual, gain, w_out, w_gate, w_up, w_down):
    vmem = pl.BlockSpec(memory_space=pltpu.VMEM)
    anywhere = pl.BlockSpec(memory_space=pl.ANY)
    dma = pltpu.SemaphoreType.DMA
    return pl.pallas_call(
        layer,
        out_shape=jax.ShapeDtypeStruct((512, 128), BF16),
        in_specs=[anywhere] * 7,
        out_specs=vmem,
        scratch_shapes=[
            pltpu.VMEM((2, 2, 4, 4, 256, 128), BF16),
            pltpu.VMEM((4, 2, 4, 4, 256, 128), BF16),
            pltpu.VMEM((4, 2, 4, 4, 256, 128), BF16),
            pltpu.VMEM((4, 4, 4, 256, 128), BF16),
            pltpu.VMEM((3, 4, 4, 256, 128), BF16),
            pltpu.VMEM((3, 4, 256, 128), BF16),
            pltpu.VMEM((3, 256, 128), BF16),
            pltpu.VMEM((256, 128), BF16),
            pltpu.VMEM((256, 128), BF16),
            pltpu.VMEM((256, 128), BF16),
            pltpu.VMEM((256, 128), BF16),
            pltpu.VMEM(w_out.shape, BF16),
            pltpu.VMEM(w_gate.shape, BF16),
            pltpu.VMEM(w_up.shape, BF16),
            pltpu.VMEM(w_down.shape, BF16),
            pltpu.VMEM((256, 128), BF16),
            pltpu.VMEM((1, D), F32),
            pltpu.VMEM((256, w_gate.shape[0]), F32),
            pltpu.VMEM((256, w_gate.shape[0]), F32),
            pltpu.VMEM((256, 128), F32),
            pltpu.VMEM((256, w_gate.shape[0]), BF16),
            pltpu.VMEM((2, 2, 128, 128), F32),
            dma((7,)),
            dma((5,)), dma((108,)), dma((3,)), dma((63,)),
            dma((6,)), dma((6,)),
            dma((3,)), dma((3,)),
        ],
        compiler_params=pltpu.CompilerParams(collective_id=0, has_side_effects=True, vmem_limit_bytes=60 << 20),
        name="layer_rest",
    )(attn, residual, gain, w_out, w_gate, w_up, w_down)


def per_device(
    queries, new_token_pairs, paged_cache_store, page_table, cache_lengths,
    out_weight, residual, norm_gain, gate_weight, up_weight, down_weight,
):
    attn = attention(queries, new_token_pairs, paged_cache_store, page_table, cache_lengths)
    return rest(attn, residual, norm_gain.reshape(1, D), out_weight, gate_weight, up_weight, down_weight)


def solution(mesh):
    in_specs = (
        P(("grp", "tp"), None, "sec"),
        P(("grp", "tp"), None, None, "sec"),
        P(("grp", "tp"), None, None, "sec"),
        P(("grp", "tp"), None),
        P(("grp", "tp")),
        P("sec", ("grp", "tp")),
        P(None, ("grp", "tp")),
        P(),
        P(("sec", "grp", "tp"), None),
        P(("sec", "grp", "tp"), None),
        P(("sec", "grp", "tp"), None),
    )
    out_specs = P(None, ("grp", "tp"))
    return jax.shard_map(
        per_device, mesh=mesh, in_specs=in_specs, out_specs=out_specs, check_vma=False
    )
```

```python
import functools
import math

import jax
import jax.numpy as jnp
from jax import lax
from jax.experimental import pallas as pl
from jax.experimental.pallas import tpu as pltpu
from jax.sharding import PartitionSpec as P

D = 8192
HEAD_SIZE = 128
EPS = 1e-05
MESH = pl.DeviceIdType.MESH
F32 = jnp.float32
BF16 = jnp.bfloat16

PAGE = 64
CHUNK_PAGES = 8
CHUNK = PAGE * CHUNK_PAGES
MAXLEN = 3072
REQS = 2
KV_HEADS = 4
GROUP = 8
TOKENS = 4
NEW_ROWS = REQS * TOKENS * 2

PARTS = ((0, 64), (64, 96), (160, 96))
HALF_PARTS = (((0, 48), (48, 48), (96, 32)), ((128, 32), (160, 48), (208, 48)))
HALF = 128
ORDERS = (("x", "y", "z"), ("y", "z", "x"), ("z", "x", "y"))
LAYOUT = ("z", "y", "x")


def attend(table, lengths, q_ref, new_ref, kv_ref, out_ref, flat, new_flat, s_buf, acc, o32, sems, new_sems):
    kv_rows = kv_ref.reshape(kv_ref.shape[0], 2 * PAGE, KV_HEADS * HEAD_SIZE)
    new_rows = new_ref.reshape(NEW_ROWS, KV_HEADS * HEAD_SIZE)
    factor = 1.0 / math.sqrt(HEAD_SIZE)
    rows = GROUP * TOKENS
    queries = KV_HEADS * rows
    nt = (((1,), (1,)), ((), ()))

    new_copies = []
    new_flat[:, pl.ds(NEW_ROWS, 128 - NEW_ROWS), :] = jnp.zeros((KV_HEADS, 128 - NEW_ROWS, HEAD_SIZE), BF16)
    for h in range(KV_HEADS):
        copy = pltpu.make_async_copy(
            new_rows.at[:, pl.ds(h * HEAD_SIZE, HEAD_SIZE)], new_flat.at[h, pl.ds(0, NEW_ROWS)], new_sems.at[h]
        )
        copy.start()
        new_copies.append(copy)

    for r in range(REQS):
        chunks = (lengths[r] + CHUNK - 1) // CHUNK

        def start(p, _, r=r):
            page = table[r, p]
            for h in range(KV_HEADS):
                pltpu.make_async_copy(
                    kv_rows.at[page, :, pl.ds(h * HEAD_SIZE, HEAD_SIZE)],
                    flat.at[h, r, pl.ds(pl.multiple_of(p * 2 * PAGE, 2 * PAGE), 2 * PAGE)],
                    sems.at[r, p // CHUNK_PAGES],
                ).start()
            return 0

        lax.fori_loop(0, chunks * CHUNK_PAGES, start, 0)

    stacked = []
    for r in range(REQS):
        wide = q_ref[r].astype(F32)
        blocks = []
        for h in range(KV_HEADS):
            q = jnp.concatenate(
                [wide[:, (h * GROUP + g) * HEAD_SIZE : (h * GROUP + g + 1) * HEAD_SIZE] for g in range(GROUP)], axis=0
            ).astype(BF16)
            zero = jnp.zeros_like(q)
            blocks.append(jnp.concatenate([q if k == h else zero for k in range(KV_HEADS)], axis=1))
        stacked.append(jnp.concatenate(blocks, axis=0))

    def pairs(r, first, count):
        return jnp.concatenate([flat[h, r, pl.ds(first, count), :] for h in range(KV_HEADS)], axis=1)

    col = lax.broadcasted_iota(jnp.int32, (queries, 128), 1)
    row = lax.broadcasted_iota(jnp.int32, (queries, 128), 0)
    wide_col = lax.broadcasted_iota(jnp.int32, (8, 2 * CHUNK), 1)
    place = jnp.where(wide_col % 2 == 0, wide_col, 2 * MAXLEN)[:1]

    for copy in new_copies:
        copy.wait()
    new_pairs = jnp.concatenate([new_flat[h] for h in range(KV_HEADS)], axis=1)
    fresh = []
    for r in range(REQS):
        s = lax.dot_general(stacked[r], new_pairs, nt, preferred_element_type=F32)
        token = (col - r * 2 * TOKENS) // 2
        live = (col % 2 == 0) & (col >= r * 2 * TOKENS) & (token <= row % TOKENS)
        fresh.append(jnp.where(live, s * factor, -jnp.inf))

    for r in range(REQS):
        length = lengths[r]
        chunks = (length + CHUNK - 1) // CHUNK
        q = stacked[r]

        def score(c, peak, r=r, q=q, length=length):
            here = flat.at[:, r, pl.ds(pl.multiple_of(c * 2 * CHUNK, 2 * CHUNK), 2 * CHUNK)]
            pltpu.make_async_copy(
                here, here, sems.at[r, c]
            ).wait()
            s = lax.dot_general(
                q, pairs(r, pl.multiple_of(c * 2 * CHUNK, 2 * CHUNK), 2 * CHUNK), nt, preferred_element_type=F32
            )
            s = jnp.where(place < 2 * (length - c * CHUNK), s * factor, -jnp.inf)
            s_buf[c] = s
            for t in range(2 * CHUNK // 128):
                peak = jnp.maximum(peak, s[:, t * 128 : (t + 1) * 128])
            return peak

        peak = jnp.max(lax.fori_loop(0, chunks, score, fresh[r]), axis=1, keepdims=True)

        w = jnp.exp(fresh[r] - peak)
        acc[...] = jnp.dot(
            pltpu.roll(w, 1, 1).astype(BF16), new_pairs, preferred_element_type=F32
        )

        def weigh(c, total, r=r, peak=peak):
            moved = []
            for t in range(2 * CHUNK // 128):
                w = jnp.exp(s_buf[c, :, t * 128 : (t + 1) * 128] - peak)
                total = total + w
                moved.append(pltpu.roll(w, 1, 1).astype(BF16))
            acc[...] += jnp.dot(
                jnp.concatenate(moved, axis=1),
                pairs(r, pl.multiple_of(c * 2 * CHUNK, 2 * CHUNK), 2 * CHUNK),
                preferred_element_type=F32,
            )
            return total

        total = jnp.sum(lax.fori_loop(0, chunks, weigh, w), axis=1, keepdims=True)
        for h in range(KV_HEADS):
            here = slice(h * rows, (h + 1) * rows)
            out = acc[here, h * HEAD_SIZE : (h + 1) * HEAD_SIZE] / total[here]
            for g in range(GROUP):
                o32[h * GROUP + g, r * TOKENS : (r + 1) * TOKENS, :] = out[g * TOKENS : (g + 1) * TOKENS]
    out_ref[...] = o32[...].reshape(KV_HEADS * GROUP * REQS * TOKENS, HEAD_SIZE).astype(BF16)


def attention(queries, new_token_pairs, paged_cache_store, page_table, cache_lengths):
    smem = pl.BlockSpec(memory_space=pltpu.SMEM)
    vmem = pl.BlockSpec(memory_space=pltpu.VMEM)
    anywhere = pl.BlockSpec(memory_space=pl.ANY)
    return pl.pallas_call(
        attend,
        out_shape=jax.ShapeDtypeStruct((256, HEAD_SIZE), BF16),
        in_specs=[smem, smem, vmem, anywhere, anywhere],
        out_specs=vmem,
        scratch_shapes=[
            pltpu.VMEM((KV_HEADS, REQS, 2 * MAXLEN, HEAD_SIZE), BF16),
            pltpu.VMEM((KV_HEADS, 128, HEAD_SIZE), BF16),
            pltpu.VMEM((MAXLEN // CHUNK, KV_HEADS * GROUP * TOKENS, 2 * CHUNK), F32),
            pltpu.VMEM((KV_HEADS * GROUP * TOKENS, KV_HEADS * HEAD_SIZE), F32),
            pltpu.VMEM((KV_HEADS * GROUP, REQS * TOKENS, HEAD_SIZE), F32),
            pltpu.SemaphoreType.DMA((REQS, MAXLEN // CHUNK)),
            pltpu.SemaphoreType.DMA((KV_HEADS,)),
        ],
        compiler_params=pltpu.CompilerParams(vmem_limit_bytes=58 << 20),
        name="paged_attention",
    )(page_table, cache_lengths, queries, new_token_pairs, paged_cache_store)


def split(at, size):
    first = next(a for a in LAYOUT if isinstance(at[a], slice))
    half = size[first] // 2
    return first, ({**at, first: pl.ds(0, half)}, {**at, first: pl.ds(half, half)})


def drain(buf, tiles, sem):
    blocks = buf.reshape(-1, 256, 128)
    rows = next(r for r in range(256, 0, -16) if tiles * 16 % r == 0 and tiles * 16 // r <= blocks.shape[0])
    bulk = blocks.at[pl.ds(0, tiles * 16 // rows), pl.ds(0, rows)]
    pltpu.make_async_copy(bulk, bulk, sem).wait()


class Gather:
    def __init__(self, net, buf, coord, offsets, parts, sems, base):
        self.net, self.buf, self.coord, self.offsets, self.parts = net, buf, coord, offsets, parts
        self.size = {"z": buf.shape[0], "y": buf.shape[2], "x": buf.shape[3]}
        self.send, self.recv, self.fsend, self.frecv = sems
        self.turn, self.base = base, base * 12
        self.sent = self.passed = 0
        self.due = [[0] * 4 for _ in parts]
        self.held = [dict(coord) for _ in parts]
        self.pending = [[] for _ in parts]

    def region(self, at, rows):
        return self.buf.at[at["z"], self.net.core, at["y"], at["x"], pl.ds(*rows)]

    def forward(self, at, rows):
        part = self.region(at, rows)
        self.net.copy(part, part, self.fsend.at[self.turn], self.frecv.at[self.turn], self.net.sibling).start()
        self.passed += math.prod(part.shape) // 2048

    def push(self, p, stage, at, axis, k):
        block = self.region(at, self.parts[p])
        recv = self.recv.at[self.base + p * 4 + stage]
        self.net.copy(block, block, self.send.at[self.turn], recv, self.net.shifted(axis, k)).start()
        tiles = math.prod(block.shape) // 2048
        self.sent += tiles
        self.due[p][stage] += tiles

    def came(self, axis, k):
        return (self.coord[axis] + 4 - k) % 4 if self.size[axis] == 4 else 1 - self.coord[axis]

    def ring(self, p):
        return len(self.offsets[ORDERS[p][2]]) == 3

    def launch(self, p, stage):
        axis = ORDERS[p][stage]
        held = self.held[p]
        if stage == 2 and self.ring(p):
            _, (low, high) = split(held, self.size)
            for slot, at, k in ((2, low, 1), (2, high, 3), (3, high, 1), (3, low, 3)):
                self.push(p, slot, at, axis, k)
                self.pending[p].append(({**at, axis: self.came(axis, k)}, k))
            return
        for k in self.offsets[axis]:
            self.push(p, stage, held, axis, k)
            self.pending[p].append(({**held, axis: self.came(axis, k)}, k))

    def start(self):
        for p in range(3):
            self.launch(p, 0)

    def land(self, p, count, stage):
        arrived, self.pending[p] = self.pending[p][:count], self.pending[p][count:]
        drain(self.buf, self.due[p][stage], self.recv.at[self.base + p * 4 + stage])
        return arrived

    def step(self, stage):
        for p in range(3):
            arrived = self.land(p, len(self.pending[p]), 3 if stage == 2 and self.ring(p) else stage)
            if stage < 2:
                axis = ORDERS[p][stage]
                self.held[p] = {**self.held[p], axis: slice(None)}
                self.launch(p, stage + 1)
            else:
                for at, _ in arrived:
                    self.forward(at, self.parts[p])
        if stage == 1:
            for p in range(3):
                self.forward(self.held[p], self.parts[p])

    def relay(self):
        landed = []
        for p in range(3):
            if not self.ring(p):
                continue
            axis = ORDERS[p][2]
            arrived = self.land(p, 2, 2)
            for at, k in arrived:
                self.push(p, 3, at, axis, k)
                self.pending[p].append(({**at, axis: self.came(axis, 2)}, k))
            landed.append((p, arrived))
        for p, arrived in landed:
            for at, _ in arrived:
                self.forward(at, self.parts[p])

    def finish(self):
        drain(self.buf, self.passed, self.frecv.at[self.turn])

    def drain(self):
        drain(self.buf, self.sent, self.send.at[self.turn])
        drain(self.buf, self.passed, self.fsend.at[self.turn])


class Scatter:
    def __init__(self, net, Q, landing, parts, sems, base):
        self.net, self.Q, self.landing, self.parts = net, Q, landing, parts
        self.send, self.recv = sems
        self.turn, self.base = base, base * 12
        self.due = [[0] * 4 for _ in parts]
        self.sent = 0

    def push(self, p, stage, src, dst, axis, k):
        recv = self.recv.at[self.base + p * 4 + stage]
        self.net.copy(src, dst, self.send.at[3 + self.turn], recv, self.net.shifted(axis, k)).start()
        tiles = math.prod(src.shape) // 2048
        self.sent += tiles
        self.due[p][stage] += tiles

    def land(self, p, stage):
        drain(self.Q, self.due[p][stage], self.recv.at[self.base + p * 4 + stage])

    def part(self, p, at):
        return self.Q.at[at["z"], self.net.core, at["y"], at["x"], pl.ds(*self.parts[p])]

    def first(self, p):
        order = ORDERS[p][::-1]
        axis = order[0]
        whole = {a: (self.net.me[a] if a == axis else slice(None)) for a in LAYOUT}
        return axis, split(whole, {a: 4 for a in LAYOUT})[1], [a for a in LAYOUT if a != axis]

    def start(self, p):
        axis, halves, left = self.first(p)
        rows = pl.ds(*self.parts[p])
        me = self.net.me[axis]
        for slot, half, away, k, land in ((0, 0, 2, 1, 2), (0, 1, 2, 3, 2), (1, 1, 1, 1, 0), (1, 0, 3, 3, 1)):
            at = {**halves[half], axis: (me + away) % 4}
            dst = self.landing[0].at[land, pl.ds(half * 2, 2), :, rows]
            self.push(p, slot, self.part(p, at), dst, axis, k)

    def relay(self):
        for p in range(3):
            axis, halves, left = self.first(p)
            rows = pl.ds(*self.parts[p])
            me = self.net.me[axis]
            self.land(p, 0)
            for slot, half, k, land in ((1, 0, 1, 0), (1, 1, 3, 1)):
                target = (me + k) % 4

                def add(i, _, half=half, rows=rows, target=target, axis=axis, left=left):
                    where = (half * 2 + i // 4, i % 4)
                    at = {axis: target, **dict(zip(left, where))}
                    got = self.landing[0][2, where[0], where[1], rows].astype(F32)
                    spot = (at["z"], self.net.core, at["y"], at["x"], rows)
                    self.Q[spot] = (self.Q[spot].astype(F32) + got).astype(BF16)
                    return 0

                lax.fori_loop(0, 8, add, 0)
                dst = self.landing[0].at[land, pl.ds(half * 2, 2), :, rows]
                self.push(p, slot, self.part(p, {**halves[half], axis: target}), dst, axis, k)

    def launch(self, p, stage):
        order = ORDERS[p][::-1]
        axis, left = order[stage], order[stage + 1 :]
        me = self.net.me
        for k in (1, 2, 3):
            at = {a: (slice(None) if a in left else me[a]) for a in LAYOUT}
            at[axis] = (me[axis] + k) % 4
            dst = self.landing[stage].at[(k - 1, *(slice(None),) * len(left), pl.ds(*self.parts[p]))]
            self.push(p, stage + 1, self.part(p, at), dst, axis, k)

    def step(self, stage):
        for p in range(3):
            order = ORDERS[p][::-1]
            left = [a for a in LAYOUT if a in order[stage + 1 :]]
            rows = pl.ds(*self.parts[p])
            me, core, Q = self.net.me, self.net.core, self.Q
            land = self.landing[stage]
            self.land(p, stage + 1)
            if stage == 2:
                continue

            def add(i, _, left=left, rows=rows, land=land):
                where = (i // 4, i % 4) if stage == 0 else (i,)
                at = {**me, **dict(zip(left, where))}
                total = Q[at["z"], core, at["y"], at["x"], rows].astype(F32)
                for k in range(2 if stage == 0 else 3):
                    got = land[k, where[0], where[1], rows] if stage == 0 else land[k, where[0], rows]
                    total = total + got.astype(F32)
                Q[at["z"], core, at["y"], at["x"], rows] = total.astype(BF16)
                return 0

            lax.fori_loop(0, 16 if stage == 0 else 4, add, 0)
            self.launch(p, stage + 1)

    def drain(self):
        drain(self.Q, self.sent, self.send.at[3 + self.turn])


class Net:
    def __init__(self):
        sec, grp, tp = lax.axis_index("sec"), lax.axis_index("grp"), lax.axis_index("tp")
        self.sec, self.zh, self.core = sec, grp // 2, grp % 2
        self.me = {"z": self.zh * 2 + sec, "y": tp // 4, "x": tp % 4}
        self.sibling = self.device(self.me, 1 - self.core)
        self.partner = self.device({**self.me, "z": self.zh * 2 + (1 - sec)}, self.core)

    def device(self, at, core):
        return (at["z"] % 2, (at["z"] // 2) * 2 + core, at["y"] * 4 + at["x"])

    def shifted(self, axis, k):
        return self.device({**self.me, axis: (self.me[axis] + k) % 4}, self.core)

    def copy(self, src, dst, send, recv, to):
        return pltpu.make_async_remote_copy(src, dst, send, recv, device_id=to, device_id_type=MESH)


def layer(
    attn, residual, gain, w_out, w_gate, w_up, w_down, out_ref,
    A, X, Q, RC, R1, R2, R3, sec_in, sec_out, fin_in, fin_out,
    wo, wg, wu, wd, res, scales, acc_g, acc_u, acc_s, hidden, mixed,
    w_sem, s1, r1, f1s, f1r, cs, cr, xs, xr,
):
    net = Net()
    sec, zh, c, me = net.sec, net.zh, net.core, net.me

    barrier = pltpu.get_barrier_semaphore()
    for axis in LAYOUT:
        for k in (1, 2, 3):
            pl.semaphore_signal(barrier, 1, device_id=net.shifted(axis, k), device_id_type=MESH)
    pl.semaphore_signal(barrier, 1, device_id=net.sibling, device_id_type=MESH)

    half_rows = pl.ds(pl.multiple_of(sec * 256, 256), 256)
    loads = [
        pltpu.make_async_copy(src, dst, w_sem.at[i])
        for i, (src, dst) in enumerate(
            (
                (w_out, wo), (w_gate, wg), (w_up, wu), (w_down, wd),
                (attn, A.at[zh, c, me["y"], me["x"]]), (residual.at[half_rows], res), (gain, scales),
            )
        )
    ]
    for i in (4, 5, 6, 0, 1, 2, 3):
        loads[i].start()
    pl.semaphore_wait(barrier, 10)

    loads[4].wait()
    every = (1, 2, 3)
    rows_gather = Gather(
        net, A, {"z": zh, "y": me["y"], "x": me["x"]}, {"z": (2,), "y": every, "x": every},
        PARTS, (s1, r1, f1s, f1r), 0,
    )
    rows_gather.start()

    def scale_weights():
        for i in (1, 2, 6):
            loads[i].wait()

        def scale(i, _):
            cols = pl.ds(pl.multiple_of(i * 512, 512), 512)
            g = scales[:, cols]
            wg[:, cols] = (wg[:, cols].astype(F32) * g).astype(BF16)
            wu[:, cols] = (wu[:, cols].astype(F32) * g).astype(BF16)
            return 0

        lax.fori_loop(0, D // 512, scale, 0)

    rows_gather.step(0)
    rows_gather.step(1)
    rows_gather.relay()
    rows_gather.step(2)

    loads[0].wait()

    def project(core):
        total = jnp.zeros((512, 256), F32)
        for j in range(0, 16, 2):
            lhs = jnp.concatenate(
                [A[:, core, :, :, (j + t) * 16 : (j + t + 1) * 16, :].reshape(512, 128) for t in range(2)], axis=1
            )
            rhs = jnp.concatenate(
                [
                    jnp.concatenate(
                        [wo[(2 * (j + t) + u) * 128 : (2 * (j + t) + u + 1) * 128, :] for u in range(2)], axis=1
                    )
                    for t in range(2)
                ],
                axis=0,
            )
            total = total + jnp.dot(lhs, rhs, preferred_element_type=F32)
        total = total.reshape(32, 2, 8, 256)
        mixed[:, core] = (total[:, 0, :, :128] + total[:, 1, :, 128:]).reshape(2, 128, 128)

    project(c)
    rows_gather.finish()
    project(1 - c)

    sec_out[...] = mixed[1 - sec].reshape(256, 128).astype(BF16)
    swap = net.copy(sec_out, sec_in, xs.at[0], xr.at[0], net.partner)
    swap.start()
    loads[5].wait()
    own = res[...].astype(F32)
    swap.wait_recv()
    X[me["z"], c, me["y"], me["x"]] = (
        own + (mixed[sec].reshape(256, 128) + sec_in[...].astype(F32))
    ).astype(BF16)

    gathers = [
        Gather(
            net, X, me, {"z": every, "y": every, "x": every}, HALF_PARTS[h], (s1, r1, f1s, f1r), h + 1
        )
        for h in range(2)
    ]
    scatters = [Scatter(net, Q, (R1, R2, R3), HALF_PARTS[h], (s1, r1), h) for h in range(2)]

    def ffn_in(h, core, first):
        rows = pl.ds(h * HALF, HALF)
        if first:
            acc_g[...] = jnp.zeros_like(acc_g)
            acc_u[...] = jnp.zeros_like(acc_u)
            acc_s[...] = jnp.zeros_like(acc_s)

        def body(hi, _):
            cols = pl.ds(pl.multiple_of((hi * 2 + core) * 2048, 2048), 2048)
            halves = []
            for lo in range(2):
                blocks = [X[hi * 2 + lo, core, b // 4, b % 4, rows] for b in range(16)]
                squares = acc_s[lo * HALF : (lo + 1) * HALF]
                for b in blocks:
                    wide = b.astype(F32)
                    squares = squares + wide * wide
                acc_s[lo * HALF : (lo + 1) * HALF] = squares
                halves.append(jnp.concatenate(blocks, axis=1))
            lhs = jnp.concatenate(halves, axis=0)
            nt = (((1,), (1,)), ((), ()))
            acc_g[...] += lax.dot_general(lhs, wg[:, cols], nt, preferred_element_type=F32)
            acc_u[...] += lax.dot_general(lhs, wu[:, cols], nt, preferred_element_type=F32)
            return 0

        lax.fori_loop(0, 2, body, 0)

    def activate():
        inv = lax.rsqrt(jnp.sum(acc_s[...], axis=1, keepdims=True) / D + EPS)
        gate = acc_g[...] * inv
        hidden[...] = (gate / (1.0 + jnp.exp(-gate)) * (acc_u[...] * inv)).astype(BF16)

    def core_copy(h, p):
        rows = pl.ds(*HALF_PARTS[h][p])
        return net.copy(
            Q.at[:, 1 - c, :, :, rows], RC.at[:, :, :, rows], cs.at[h * 3 + p], cr.at[h * 3 + p], net.sibling
        )

    def ffn_out(h):
        rows = pl.ds(h * HALF, HALF)

        def tile(core, hi):
            cols = pl.ds(pl.multiple_of((hi * 2 + core) * 2048, 2048), 2048)
            part = jnp.dot(hidden[...], wd[:, cols], preferred_element_type=F32)
            for lo in range(2):
                for y in range(4):
                    for x in range(4):
                        Q[hi * 2 + lo, core, y, x, rows] = part[
                            lo * HALF : (lo + 1) * HALF, (y * 4 + x) * 128 : (y * 4 + x + 1) * 128
                        ].astype(BF16)

        for hi in range(2):
            tile(1 - c, hi)
        swaps = [core_copy(h, p) for p in range(3)]
        for copy in swaps:
            copy.start()
        for hi in range(2):
            tile(c, hi)
        for p in range(3):
            here = pl.ds(*HALF_PARTS[h][p])
            swaps[p].wait_recv()

            def add_sibling(i, _, here=here):
                z, y = i // 4, i % 4
                for x in range(4):
                    Q[z, c, y, x, here] = (Q[z, c, y, x, here].astype(F32) + RC[z, y, x, here].astype(F32)).astype(
                        BF16
                    )
                return 0

            lax.fori_loop(0, 16, add_sibling, 0)
            scatters[h].start(p)
        return swaps

    def close(h):
        rows = pl.ds(h * HALF, HALF)
        total = X[me["z"], c, me["y"], me["x"], rows].astype(F32)
        ffn = Q[me["z"], c, me["y"], me["x"], rows].astype(F32)
        for k in range(3):
            ffn = ffn + R3[k, rows].astype(F32)
        done = (total + ffn).astype(BF16)
        fin_out[rows] = done
        last = net.copy(fin_out.at[rows], fin_in.at[rows], xs.at[1 + h], xr.at[1 + h], net.partner)
        last.start()
        out_ref[pl.ds(pl.multiple_of(sec * 256 + h * HALF, HALF), HALF), :] = done
        return last

    g0, g1 = gathers
    t0, t1 = scatters
    g0.start()
    rows_gather.drain()
    g0.step(0)
    g1.start()
    g0.step(1)
    g1.step(0)
    g0.relay()
    g1.step(1)
    scale_weights()
    g0.step(2)
    ffn_in(0, c, True)
    g0.finish()
    ffn_in(0, 1 - c, False)
    g1.relay()
    activate()
    loads[3].wait()
    swaps = ffn_out(0)
    g1.step(2)
    ffn_in(1, c, True)
    g1.finish()
    t0.relay()
    ffn_in(1, 1 - c, False)
    activate()
    g0.drain()
    swaps += ffn_out(1)
    t0.step(0)
    t1.relay()
    g1.drain()
    for copy in swaps:
        copy.wait_send()
    t0.step(1)
    t1.step(0)
    t0.step(2)
    last0 = close(0)
    t0.drain()
    t1.step(1)
    t1.step(2)
    last1 = close(1)
    swap.wait_send()
    t1.drain()
    last0.wait()
    last1.wait()
    out_ref[pl.ds(pl.multiple_of((1 - sec) * 256, 256), 256), :] = fin_in[...]


def rest(attn, residual, gain, w_out, w_gate, w_up, w_down):
    vmem = pl.BlockSpec(memory_space=pltpu.VMEM)
    anywhere = pl.BlockSpec(memory_space=pl.ANY)
    dma = pltpu.SemaphoreType.DMA
    return pl.pallas_call(
        layer,
        out_shape=jax.ShapeDtypeStruct((512, 128), BF16),
        in_specs=[anywhere] * 7,
        out_specs=vmem,
        scratch_shapes=[
            pltpu.VMEM((2, 2, 4, 4, 256, 128), BF16),
            pltpu.VMEM((4, 2, 4, 4, 256, 128), BF16),
            pltpu.VMEM((4, 2, 4, 4, 256, 128), BF16),
            pltpu.VMEM((4, 4, 4, 256, 128), BF16),
            pltpu.VMEM((3, 4, 4, 256, 128), BF16),
            pltpu.VMEM((3, 4, 256, 128), BF16),
            pltpu.VMEM((3, 256, 128), BF16),
            pltpu.VMEM((256, 128), BF16),
            pltpu.VMEM((256, 128), BF16),
            pltpu.VMEM((256, 128), BF16),
            pltpu.VMEM((256, 128), BF16),
            pltpu.VMEM(w_out.shape, BF16),
            pltpu.VMEM(w_gate.shape, BF16),
            pltpu.VMEM(w_up.shape, BF16),
            pltpu.VMEM(w_down.shape, BF16),
            pltpu.VMEM((256, 128), BF16),
            pltpu.VMEM((1, D), F32),
            pltpu.VMEM((256, w_gate.shape[0]), F32),
            pltpu.VMEM((256, w_gate.shape[0]), F32),
            pltpu.VMEM((256, 128), F32),
            pltpu.VMEM((256, w_gate.shape[0]), BF16),
            pltpu.VMEM((2, 2, 128, 128), F32),
            dma((7,)),
            dma((5,)), dma((36,)), dma((3,)), dma((3,)),
            dma((6,)), dma((6,)),
            dma((3,)), dma((3,)),
        ],
        compiler_params=pltpu.CompilerParams(collective_id=0, has_side_effects=True, vmem_limit_bytes=60 << 20),
        name="layer_rest",
    )(attn, residual, gain, w_out, w_gate, w_up, w_down)


def per_device(
    queries, new_token_pairs, paged_cache_store, page_table, cache_lengths,
    out_weight, residual, norm_gain, gate_weight, up_weight, down_weight,
):
    attn = attention(queries, new_token_pairs, paged_cache_store, page_table, cache_lengths)
    return rest(attn, residual, norm_gain.reshape(1, D), out_weight, gate_weight, up_weight, down_weight)


def solution(mesh):
    in_specs = (
        P(("grp", "tp"), None, "sec"),
        P(("grp", "tp"), None, None, "sec"),
        P(("grp", "tp"), None, None, "sec"),
        P(("grp", "tp"), None),
        P(("grp", "tp")),
        P("sec", ("grp", "tp")),
        P(None, ("grp", "tp")),
        P(),
        P(("sec", "grp", "tp"), None),
        P(("sec", "grp", "tp"), None),
        P(("sec", "grp", "tp"), None),
    )
    out_specs = P(None, ("grp", "tp"))
    return jax.shard_map(
        per_device, mesh=mesh, in_specs=in_specs, out_specs=out_specs, check_vma=False
    )
```
